256 devices in a mesh: ctx: 32 (over x, y, core), tp: 4 (over z_lo), sec: 2 (over z_hi).
Axes of the slice: x: 4, y: 4, z: 8 (z_hi: 2, z_lo: 4; z = z_hi * 4 + z_lo), core: 2. Of those that a mesh axis runs over, the one named last changes fastest.
Arguments:
- queries: bfloat16 [2, 2048, 8192], P('sec', 'ctx', 'tp'), may hold values from -16 to 16
- keys: bfloat16 [2, 2048, 1024], P('sec', 'ctx', 'tp'), may hold values from -6 to 6
- values: bfloat16 [2, 2048, 1024], P('sec', 'ctx', 'tp'), may hold values from -24 to 24
- page_owner: int32 [256, 2], replicated, may hold values from 0 to 31, all different within a row; in each aligned block of 8 rows (0 to 7, 8 to 15, ...) at most 2 rows name the same one
- lengths: int32 [32, 16], P('ctx'), may hold values from 1 to 512, 3968 in all within a row
- page_table: int32 [32, 512], P('ctx'), may hold values from 0 to 511, as said below
- group_cache_keys: bfloat16 [16384, 8, 1024], P('ctx', None, 'tp'), may hold values from -6 to 6
- group_cache_values: bfloat16 [16384, 8, 1024], P('ctx', None, 'tp'), may hold values from -24 to 24
Outputs:
- attended: bfloat16 [2, 2048, 8192], P('sec', 'ctx', 'tp')
The draws below stay inside these ranges and needn't reach their ends.
Inputs may be any that keep to these rules, and one draw needn't show every extreme that they name: `page_owner`: each row names 2 different decode groups; within the 8 rows of one prompt index no group is named more than 2 times. Each group's 16 lengths sum to 3968 and the largest of them is 512. `page_table`: each row names every page of 0 to 511 once.
All inputs are finite; a program needn't handle non-finite values.
Results may differ from the reference program's by a relative error of at most 0.0034.
Values may be sent and summed in bfloat16 or wider, within the bound.
No kernel may reach another device: no remote copies, remote signals or barrier semaphores. Data moves between devices by JAX's collectives and lax.ppermute only.
A program may use at most 64 MiB of HBM per device.

```python
import math
import jax
import jax.numpy as jnp
import numpy as np
from jax import lax

QUERY_HEADS = 64
KEY_VALUE_HEADS = 8
HEAD_WIDTH = 128
DECODE_STEPS = 4
PAGE_TOKENS = 8
TOP = 2
MAXP = 64
GROUP_PAGES = 512
PROMPT_TOKENS = 2048
SEQ_DEV = 16
PPD = 8
PROMPT_PAGES = 256
MOST = 2
HAND = 64
LONGEST_CONTEXT = 512
CACHED = 3968
N_CTX = 32


def draw_keys(key, part):
    key = jax.random.fold_in(key, 11)
    return jnp.clip(jax.random.normal(key, (2, PROMPT_TOKENS, KEY_VALUE_HEADS * HEAD_WIDTH), jnp.float32), -6.0, 6.0).astype(jnp.bfloat16)


def draw_queries(key, part):
    key = jax.random.fold_in(key, 12)
    return jnp.clip(2.0 * jax.random.normal(key, (2, PROMPT_TOKENS, QUERY_HEADS * HEAD_WIDTH), jnp.float32), -12.0, 12.0).astype(jnp.bfloat16)


def draw_page_table(key, part):
    key = jax.random.fold_in(key, 13)
    front_key, back_key = jax.random.split(key, 2)
    front_keys = jax.random.split(front_key, N_CTX)
    back_keys = jax.random.split(back_key, N_CTX)
    front = jax.vmap(lambda one_key: jax.random.permutation(one_key, jnp.arange(HAND, dtype=jnp.int32)))(front_keys)
    back = jax.vmap(lambda one_key: jax.random.permutation(one_key, jnp.arange(HAND, GROUP_PAGES, dtype=jnp.int32)))(back_keys)
    return jnp.concatenate([front, back], axis=1).astype(jnp.int32)


def steps_of(stream_key, shape, cuts, least, largest):
    level = 1.0
    for axis_at, blocks in cuts:
        steps = jax.random.uniform(jax.random.fold_in(jax.random.fold_in(stream_key, 6), axis_at), (blocks,), jnp.float32, least / len(cuts), largest / len(cuts))
        level = level * jnp.repeat(jnp.exp(steps), shape[axis_at] // blocks).reshape((-1,) + (1,) * (len(shape) - 1 - axis_at))
    return level


def length_profile(number_of, total, most, skew):
    portions = [(1 << 20) // math.isqrt(standing ** skew) + 1 for standing in range(2, number_of + 1)]
    surplus, given = total - most - (number_of - 1), [1] * (number_of - 1)
    while surplus > 0:
        free = [i for i in range(number_of - 1) if given[i] < most]
        whole, budget = sum([portions[i] for i in free]), surplus
        for i in free:
            addition = min(most - given[i], max(1, budget * portions[i] // whole), surplus)
            given[i] = given[i] + addition
            surplus = surplus - addition
    return np.array([most] + given)


def ragged_sizes(rng, number_of, total, most, lean):
    if number_of == 2:
        one = jax.random.randint(rng, (), max(1, total - most), min(most, total - 1) + 1)
        return jnp.stack([one, total - one])
    sizes = jnp.asarray(length_profile(number_of, total, most, lean), jnp.int32)
    twos = (number_of - 1) // 2
    source_of, taker = sizes[1:1 + 2 * twos:2], sizes[2:2 + 2 * twos:2]
    room = jnp.minimum(source_of - 1, most - taker)
    moved = jax.random.randint(jax.random.fold_in(rng, 1), (twos,), 0, 1 << 20) % (room + 1)
    sizes = sizes.at[1:1 + 2 * twos:2].set(source_of - moved).at[2:2 + 2 * twos:2].set(taker + moved)
    return sizes[jax.random.permutation(jax.random.fold_in(rng, 2), number_of)]


def deal_out(stream_key, own, number, rows, count, top, bound, lean):
    ranking = jax.random.permutation(stream_key, count)
    packed, ordinary = shares(count, rows * top, bound, lean, True), shares(count, rows * top, bound, lean, False)
    places = jnp.arange(count)

    def named(tallies, turn):
        used = int((tallies > 0).sum())
        fixed = max(1, used // 4)
        moved = fixed + (places - fixed + turn * (used - fixed)) % max(1, count - fixed)
        return jnp.zeros((count,), jnp.int32).at[ranking[jnp.where(places < fixed, places, moved)]].set(jnp.asarray(tallies, jnp.int32))

    tallies = jnp.where(number % 4 == 0, named(packed, number // 4), named(ordinary, number - number // 4 - 1))
    mixed = jax.random.permutation(jax.random.fold_in(own, 3), count)
    donor, receiver = mixed[0:count // 2 * 2:2], mixed[1:count // 2 * 2:2]
    room = jnp.minimum(tallies[donor] - 1, bound - tallies[receiver]) // 2
    room = jnp.where((donor == ranking[0]) | (receiver == ranking[0]) | (tallies[receiver] == 0), 0, jnp.maximum(room, 0))
    moved = jax.random.randint(jax.random.fold_in(own, 4), (count // 2,), 0, 1 << 20) % (room + 1)
    tallies = tallies.at[donor].add(-moved).at[receiver].add(moved)
    members = jnp.searchsorted(jnp.cumsum(tallies), jnp.arange(rows * top), side="right").astype(jnp.int32)
    listing = members.reshape(top, rows).T
    listing = listing[jax.random.permutation(jax.random.fold_in(own, 1), rows)]
    turn = jax.random.randint(jax.random.fold_in(own, 2), (rows, 1), 0, top)
    return jnp.take_along_axis(listing, (jnp.arange(top)[None, :] + turn) % top, axis=1)


def shares(count, total, bound, skew, full):
    weights = [(1 << 20) // math.isqrt(rank ** skew) + 1 for rank in range(1, count + 1)]
    largest = bound if full else min(bound, max(-(-total // count), total * weights[0] // sum(weights)))
    least = 1 if total - largest >= count - 1 else 0
    holding, surplus = [largest] + [least] * (count - 1), total - largest - least * (count - 1)
    while surplus > 0:
        candidates = [i for i in range(1, count) if holding[i] < largest] or [i for i in range(1, count) if holding[i] < bound]
        pool, remaining = sum([weights[i] for i in candidates]), surplus
        for i in candidates:
            more = min(bound - holding[i], max(1, remaining * weights[i] // pool), surplus)
            holding[i] = holding[i] + more
            surplus = surplus - more
    return np.array(holding)


def centred(own_key, dims, scale, most, cuts=(), kind=jnp.bfloat16):
    loudness = steps_of(own_key, dims, cuts, -0.22, 0.18) if cuts else 1.0
    drawn = jax.random.normal(own_key, dims, jnp.float32) * scale * loudness
    return jnp.minimum(jnp.maximum(drawn, -most), most).astype(kind)


def setup_inputs(seed: int = 0) -> dict:
    key_of = jax.random.split(jax.random.key(seed), 9)
    queries = draw_queries(jax.random.fold_in(key_of[8], 71), 0)
    keys = draw_keys(jax.random.fold_in(key_of[8], 71), 0)
    values = centred(key_of[2], (2, PROMPT_TOKENS, KEY_VALUE_HEADS * HEAD_WIDTH), 4.0, 24.0, ((0, 2), (1, 32), (2, 4)))
    page_owner_keys = jax.random.split(jax.random.fold_in(key_of[3], 1), PROMPT_PAGES // PPD)
    page_owner_turns = jax.random.permutation(jax.random.fold_in(key_of[3], 3), PROMPT_PAGES // PPD)
    page_owner = jax.vmap(lambda own, number: deal_out(jax.random.fold_in(key_of[3], 2), own, number, PPD, N_CTX, TOP, MOST, 2))(page_owner_keys, page_owner_turns).reshape((PROMPT_PAGES, TOP))
    lengths = jax.vmap(lambda own: ragged_sizes(own, SEQ_DEV, CACHED, LONGEST_CONTEXT, 2))(jax.random.split(key_of[4], N_CTX)).reshape((N_CTX, SEQ_DEV)).astype(jnp.int32)
    page_table = draw_page_table(jax.random.fold_in(key_of[8], 71), 0)
    group_cache_keys = centred(key_of[6], (N_CTX * GROUP_PAGES, PAGE_TOKENS, KEY_VALUE_HEADS * HEAD_WIDTH), 1.0, 6.0, ((0, 32), (2, 4)))
    group_cache_values = centred(key_of[7], (N_CTX * GROUP_PAGES, PAGE_TOKENS, KEY_VALUE_HEADS * HEAD_WIDTH), 4.0, 24.0, ((0, 32), (2, 4)))
    return dict(queries=queries, keys=keys, values=values, page_owner=page_owner, lengths=lengths, page_table=page_table, group_cache_keys=group_cache_keys, group_cache_values=group_cache_values)


def round_weights(weights):
    return lax.optimization_barrier(weights.astype(jnp.bfloat16)).astype(jnp.float32)


def prefill_attend(query_row_block, key_row_block, value_row_block):
    count_of_rows = query_row_block.shape[0]
    group_width = QUERY_HEADS // KEY_VALUE_HEADS
    score_scale = HEAD_WIDTH ** -0.5
    query_heads = query_row_block.reshape(count_of_rows, KEY_VALUE_HEADS, group_width, HEAD_WIDTH).transpose(1, 0, 2, 3)
    key_heads = key_row_block.reshape(count_of_rows, KEY_VALUE_HEADS, HEAD_WIDTH).transpose(1, 0, 2)
    value_heads = value_row_block.reshape(count_of_rows, KEY_VALUE_HEADS, HEAD_WIDTH).transpose(1, 0, 2)
    block_rows = math.gcd(count_of_rows, 512)
    block_count = count_of_rows // block_rows
    key_pos = jnp.arange(count_of_rows, dtype=jnp.int32)

    def one_head(pieces):
        q_one, k_one, v_one = pieces
        k_wide = k_one.astype(jnp.float32)
        v_wide = v_one.astype(jnp.float32)

        def one_block(parts):
            q_block, first_row = parts
            scores = jnp.einsum("qgd,kd->gqk", q_block.astype(jnp.float32), k_wide) * score_scale
            row_pos = first_row + jnp.arange(block_rows, dtype=jnp.int32)
            allowed = (key_pos[None, :] <= row_pos[:, None])[None]
            scores = jnp.where(allowed, scores, -jnp.inf)
            row_peak = jnp.max(scores, axis=-1, keepdims=True)
            weights = jnp.where(allowed, jnp.exp(scores - row_peak), 0.0)
            totals = jnp.sum(weights, axis=-1)
            mixed_sum = jnp.einsum("gqk,kd->gqd", round_weights(weights), v_wide)
            return (mixed_sum / totals[..., None]).transpose(1, 0, 2)

        blocks_out = lax.map(one_block, (q_one.reshape(block_count, block_rows, group_width, HEAD_WIDTH),
                                         (jnp.arange(block_count, dtype=jnp.int32) * block_rows).astype(jnp.int32)))
        return blocks_out.reshape(count_of_rows, group_width, HEAD_WIDTH)

    result = lax.map(one_head, (query_heads, key_heads, value_heads))
    return result.transpose(1, 0, 2, 3).reshape(count_of_rows, QUERY_HEADS * HEAD_WIDTH).astype(jnp.bfloat16)


def hand_over(page_owner, incoming_rows, pool_rows):
    item_count = PPD * TOP
    owner_grid = page_owner.reshape(N_CTX, item_count).astype(jnp.int32)
    dest_hits = (owner_grid[:, :, None] == jnp.arange(N_CTX, dtype=jnp.int32)[None, None, :]).astype(jnp.int32)
    before = jnp.cumsum(dest_hits, axis=1) - dest_hits
    rank_index = jnp.sum(before * dest_hits, axis=2)
    source = jnp.arange(N_CTX, dtype=jnp.int32)[:, None]
    target = owner_grid * GROUP_PAGES + source * MOST + rank_index
    page_index = source * PPD + jnp.arange(item_count, dtype=jnp.int32)[None, :] // TOP
    page_row_block = incoming_rows.reshape(PROMPT_PAGES, PAGE_TOKENS, KEY_VALUE_HEADS * HEAD_WIDTH)
    return pool_rows.at[target.reshape(-1)].set(page_row_block[page_index.reshape(-1)])


def page_slots(length_grid, page_table):
    grid = length_grid.astype(jnp.int32)
    groups = grid.shape[0]
    needed = (grid + PAGE_TOKENS - 1) // PAGE_TOKENS
    offsets = jnp.cumsum(needed, axis=1) - needed
    wanted = offsets[:, :, None] + jnp.arange(MAXP, dtype=jnp.int32)[None, None, :]
    wanted = jnp.minimum(wanted, GROUP_PAGES - 1).astype(jnp.int32)
    picked = jnp.take_along_axis(page_table.astype(jnp.int32), wanted.reshape(groups, SEQ_DEV * MAXP), axis=1)
    return picked.reshape(groups * SEQ_DEV, MAXP).astype(jnp.int32)


def decode_attend(query_row_block, key_row_block, value_row_block, seq_lengths, slot_local, cached_key_rows, cached_value_rows):
    group_width = QUERY_HEADS // KEY_VALUE_HEADS
    score_scale = HEAD_WIDTH ** -0.5
    sequence_count = query_row_block.shape[0] // DECODE_STEPS
    query_sequence = query_row_block.reshape(sequence_count, DECODE_STEPS, KEY_VALUE_HEADS, group_width, HEAD_WIDTH)
    key_sequence = key_row_block.reshape(sequence_count, DECODE_STEPS, KEY_VALUE_HEADS, HEAD_WIDTH)
    value_sequence = value_row_block.reshape(sequence_count, DECODE_STEPS, KEY_VALUE_HEADS, HEAD_WIDTH)
    pool_base = (jnp.arange(sequence_count, dtype=jnp.int32) // SEQ_DEV) * GROUP_PAGES
    slot_table = slot_local.astype(jnp.int32) + pool_base[:, None]
    cache_pos = jnp.arange(LONGEST_CONTEXT, dtype=jnp.int32)
    step_pos = jnp.arange(DECODE_STEPS, dtype=jnp.int32)
    causal = (step_pos[None, :] <= step_pos[:, None])[None, None]

    def one_seq(pieces):
        q_one, k_one, v_one, length, page_slot_row = pieces
        previous_key = cached_key_rows[page_slot_row].reshape(LONGEST_CONTEXT, KEY_VALUE_HEADS, HEAD_WIDTH).astype(jnp.float32)
        previous_value = cached_value_rows[page_slot_row].reshape(LONGEST_CONTEXT, KEY_VALUE_HEADS, HEAD_WIDTH).astype(jnp.float32)
        q_wide = q_one.astype(jnp.float32)
        live_mask = (cache_pos < length)[None, None, None, :]
        old_scores = jnp.einsum("sjgd,ljd->jgsl", q_wide, previous_key) * score_scale
        old_scores = jnp.where(live_mask, old_scores, -jnp.inf)
        new_scores = jnp.einsum("sjgd,tjd->jgst", q_wide, k_one.astype(jnp.float32)) * score_scale
        new_scores = jnp.where(causal, new_scores, -jnp.inf)
        row_peak = jnp.maximum(jnp.max(old_scores, axis=-1), jnp.max(new_scores, axis=-1))[..., None]
        old_weights = jnp.where(live_mask, jnp.exp(old_scores - row_peak), 0.0)
        new_weights = jnp.where(causal, jnp.exp(new_scores - row_peak), 0.0)
        totals = jnp.sum(old_weights, axis=-1) + jnp.sum(new_weights, axis=-1)
        mixed_sum = jnp.einsum("jgsl,ljd->jgsd", round_weights(old_weights), previous_value)
        mixed_sum = mixed_sum + jnp.einsum("jgst,tjd->jgsd", round_weights(new_weights), v_one.astype(jnp.float32))
        return (mixed_sum / totals[..., None]).transpose(2, 0, 1, 3).reshape(DECODE_STEPS, QUERY_HEADS * HEAD_WIDTH)

    result = lax.map(one_seq, (query_sequence, key_sequence, value_sequence, seq_lengths.astype(jnp.int32), slot_table))
    return result.reshape(sequence_count * DECODE_STEPS, QUERY_HEADS * HEAD_WIDTH).astype(jnp.bfloat16)


def reference(queries, keys, values, page_owner, lengths, page_table, group_cache_keys, group_cache_values):
    prompt_out = prefill_attend(queries[0], keys[0], values[0])
    new_pool_keys = hand_over(page_owner, keys[0], group_cache_keys)
    new_pool_values = hand_over(page_owner, values[0], group_cache_values)
    slot_local = page_slots(lengths, page_table)
    decode_out = decode_attend(queries[1], keys[1], values[1], lengths.reshape(-1), slot_local,
                               new_pool_keys, new_pool_values)
    return jnp.stack([prompt_out, decode_out])
```

```python
import math

import jax
import jax.numpy as jnp
import numpy as np
from jax import lax
from jax.experimental import pallas as pl
from jax.experimental.pallas import tpu as pltpu
from jax.sharding import Mesh
from jax.sharding import PartitionSpec as P

HEAD_WIDTH = 128
GROUP_WIDTH = 8
KV_HEADS = 2
ROWS = 64
QROWS = GROUP_WIDTH * ROWS
WIDTH = KV_HEADS * HEAD_WIDTH
PAGE_TOKENS = 8
PAGES = 512
HAND = 64
SEQS = 16
STEPS = 4
TOP = 2
PPD = 8
TOKENS = PAGES * PAGE_TOKENS
HAND_TOKENS = HAND * PAGE_TOKENS
CHUNK = 256
BIG = float(2**20)
TO_LOG2 = HEAD_WIDTH**-0.5 * math.log2(math.e)
SIDE = 4
AXES = ("x", "y", "c", "t", "s")
SIZES = {"x": 4, "y": 4, "c": 2, "t": 4, "s": 2}
CTX = ("x", "y", "c")
VMEM_LIMIT = 48 * 1024 * 1024
F32 = jnp.float32
BF16 = jnp.bfloat16
I32 = jnp.int32


def moved(shard, axes, target):
    sizes = [SIZES[a] for a in axes]
    pairs = []
    for source in range(math.prod(sizes)):
        place = [int(i) for i in np.unravel_index(source, sizes)]
        goal = target(*place)
        if goal is not None:
            goal = [a % b for a, b in zip(goal, sizes)]
            pairs.append((source, int(np.ravel_multi_index(goal, sizes))))
    return lax.ppermute(shard, axes if len(axes) > 1 else axes[0], pairs)


def iota(shape, axis):
    return lax.broadcasted_iota(I32, shape, axis)


def fill_queries(q_ref, qa_ref):
    hot = jnp.where(iota((QROWS, 128), 0) % ROWS == iota((QROWS, 128), 1), 1.0, 0.0).astype(BF16)
    for j in range(KV_HEADS):
        for h in range(GROUP_WIDTH):
            at = (j * GROUP_WIDTH + h) * HEAD_WIDTH
            qa_ref[j, h * ROWS : (h + 1) * ROWS, 0:HEAD_WIDTH] = q_ref[:, at : at + HEAD_WIDTH]
        qa_ref[j, :, HEAD_WIDTH:] = hot


def head_lanes(j):
    return pl.ds(pl.multiple_of(j * HEAD_WIDTH, HEAD_WIDTH), HEAD_WIDTH)


def attend(j, qa_ref, count, key_of, value_of, bias_of, s_ref, mx_ref, m_ref, acc_ref, first):
    mx_ref[...] = jnp.full((QROWS, 128), -4.0 * BIG, F32) if first else m_ref[j]

    def scores(c, carry):
        keys = jnp.concatenate([key_of(c, j), bias_of(c)], axis=1)
        s = lax.dot_general(
            qa_ref[j], keys, (((1,), (1,)), ((), ())), preferred_element_type=F32
        )
        s_ref[c] = s
        mx_ref[...] = jnp.maximum(mx_ref[...], jnp.maximum(s[:, :128], s[:, 128:]))
        return carry

    lax.fori_loop(0, count, scores, 0)
    top = jnp.broadcast_to(jnp.max(mx_ref[...], axis=1, keepdims=True), (QROWS, 128))
    if first:
        acc_ref[j] = jnp.zeros((QROWS, 2 * HEAD_WIDTH), F32)
    else:
        shrink = jnp.exp2((m_ref[j] - top) * TO_LOG2)
        acc_ref[j] = acc_ref[j] * jnp.concatenate([shrink, shrink], axis=1)
    m_ref[j] = top
    ones = jnp.ones((CHUNK, HEAD_WIDTH), BF16)

    def mix(c, carry):
        low = m_ref[j]
        weights = jnp.exp2((s_ref[c] - jnp.concatenate([low, low], axis=1)) * TO_LOG2)
        wide = jnp.concatenate([value_of(c, j), ones], axis=1)
        acc_ref[j] += jnp.dot(weights.astype(BF16), wide, preferred_element_type=F32)
        return carry

    lax.fori_loop(0, count, mix, 0)


def finish(acc_ref, out_ref):
    for j in range(KV_HEADS):
        result = (acc_ref[j, :, :HEAD_WIDTH] / acc_ref[j, :, HEAD_WIDTH:]).astype(BF16)
        for h in range(GROUP_WIDTH):
            at = (j * GROUP_WIDTH + h) * HEAD_WIDTH
            out_ref[:, at : at + HEAD_WIDTH] = result[h * ROWS : (h + 1) * ROWS]


def place():
    return lax.axis_index("x"), lax.axis_index("y"), lax.axis_index("c")


def prompt_bias(block, me):
    key_pos = block * ROWS + iota((ROWS, 128), 0)
    row_pos = me * ROWS + iota((ROWS, 128), 1)
    return jnp.where(key_pos > row_pos, -BIG, 0.0).astype(BF16)


def prompt_kernel(pieces, first, last, info_ref, q_ref, *refs):
    count = len(pieces)
    piece_refs, refs = refs[:count], refs[count:]
    if not first:
        m_in, acc_in, refs = refs[0], refs[1], refs[2:]
    if last:
        out_ref, m_ref, acc_ref = refs[0], refs[-2], refs[-1]
        refs = refs[1:-2]
    else:
        m_ref, acc_ref, refs = refs[0], refs[1], refs[2:]
    kv_ref, bias_ref, s_ref, mx_ref, qa_ref, sems = refs
    copies = [
        pltpu.make_async_copy(ref, kv_ref.at[i], sems.at[i]) for i, ref in enumerate(piece_refs)
    ]
    for copy in copies:
        copy.start()
    x, y, c = info_ref[0], info_ref[1], info_ref[2]
    me = x * 8 + y * 2 + c
    for i, (swapped, k2) in enumerate(pieces):
        core = (1 - c) if swapped else c
        for k1 in range(SIDE):
            on_x = jnp.where(core == 0, k2, k1)
            on_y = jnp.where(core == 0, k1, k2)
            block = ((x - on_x) & 3) * 8 + ((y - on_y) & 3) * 2 + core
            bias_ref[i, k1 * ROWS : (k1 + 1) * ROWS, :] = prompt_bias(block, me)
    fill_queries(q_ref, qa_ref)
    if not first:
        m_ref[...] = m_in[...]
        acc_ref[...] = acc_in[...]
    for copy in copies:
        copy.wait()

    def key_of(i, j):
        return kv_ref[i, :, 0, :, head_lanes(j)].reshape(CHUNK, HEAD_WIDTH)

    def value_of(i, j):
        return kv_ref[i, :, 1, :, head_lanes(j)].reshape(CHUNK, HEAD_WIDTH)

    def one_head(j, carry):
        attend(
            j, qa_ref, count, key_of, value_of, lambda i: bias_ref[i],
            s_ref, mx_ref, m_ref, acc_ref, first,
        )
        return carry

    lax.fori_loop(0, KV_HEADS, one_head, 0)
    if last:
        finish(acc_ref, out_ref)


STATE = [
    jax.ShapeDtypeStruct((KV_HEADS, QROWS, 128), F32),
    jax.ShapeDtypeStruct((KV_HEADS, QROWS, 2 * HEAD_WIDTH), F32),
]


def vmem():
    return pl.BlockSpec(memory_space=pltpu.VMEM)


def prompt_attend(info, q, arrays, pieces, state, last):
    count = len(pieces)
    first = state is None
    scratch = [
        pltpu.VMEM((count, SIDE, 2, ROWS, WIDTH), BF16),
        pltpu.VMEM((count, CHUNK, 128), BF16),
        pltpu.VMEM((count, QROWS, CHUNK), F32),
        pltpu.VMEM((QROWS, 128), F32),
        pltpu.VMEM((KV_HEADS, QROWS, 2 * HEAD_WIDTH), BF16),
        pltpu.SemaphoreType.DMA((count,)),
    ]
    if last:
        scratch += [pltpu.VMEM(s.shape, s.dtype) for s in STATE]
    keys = count * CHUNK

    def kernel(*refs):
        prompt_kernel(pieces, first, last, *refs)

    return pl.pallas_call(
        kernel,
        out_shape=jax.ShapeDtypeStruct((ROWS, q.shape[1]), BF16) if last else STATE,
        in_specs=[pl.BlockSpec(memory_space=pltpu.SMEM), vmem()]
        + [pl.BlockSpec(memory_space=pl.ANY)] * count
        + ([] if first else [vmem(), vmem()]),
        out_specs=vmem() if last else [vmem(), vmem()],
        scratch_shapes=scratch,
        compiler_params=pltpu.CompilerParams(vmem_limit_bytes=VMEM_LIMIT),
        cost_estimate=pl.CostEstimate(
            flops=4 * KV_HEADS * QROWS * keys * 256,
            bytes_accessed=keys * WIDTH * 4,
            transcendentals=KV_HEADS * QROWS * keys,
        ),
    )(info, q, *arrays, *(() if first else state))


POOL_CHUNKS = TOKENS // CHUNK + 1


def pool_kernel(
    info_ref, own_ref, len_ref, table_ref, owner_ref, q_ref, new_k_ref, new_v_ref, k_hbm, v_hbm,
    m_ref, acc_ref, qa_ref, hand_bias_ref, pick_ref,
    k_ref, v_ref, bias_ref, s_ref, mx_ref, sems,
):
    @pl.when(info_ref[3] == 1)
    def _():
        copies = []
        for i in range(4):
            part = pl.ds(i * (TOKENS // 4), TOKENS // 4)
            copies.append(pltpu.make_async_copy(k_hbm.at[part], k_ref.at[part], sems.at[0, i]))
            copies.append(pltpu.make_async_copy(v_hbm.at[part], v_ref.at[part], sems.at[1, i]))
        for copy in copies:
            copy.start()
        me = info_ref[0] * 8 + info_ref[1] * 2 + info_ref[2]
        fill_queries(q_ref, qa_ref)
        sequence = iota((8, 128), 1) // STEPS
        length = jnp.zeros((8, 128), I32)
        start = jnp.zeros((8, 128), I32)
        offset = jnp.int32(0)
        for s in range(SEQS):
            one = len_ref[0, s]
            length = jnp.where(sequence == s, one, length)
            start = jnp.where(sequence == s, offset, start)
            offset = offset + ((one + PAGE_TOKENS - 1) >> 3)
        length, start = length[0:1], start[0:1]
        past = iota((PAGES, 128), 0) - start
        live = jnp.where(past >= 0, jnp.clip(length - past * PAGE_TOKENS, 0, PAGE_TOKENS), 0)
        hot = jnp.where(iota((PAGES, PAGES), 0) == table_ref[...], 1.0, 0.0).astype(BF16)
        of_page = jnp.dot(hot, live.astype(F32).astype(BF16), preferred_element_type=F32)
        page = iota((HAND, PAGES), 0)
        entry = iota((HAND, PAGES), 1)
        named = jnp.where((owner_ref[...] == me) & (entry // (PPD * TOP) == page // 2), 1.0, 0.0)
        total = jnp.sum(named, axis=1, keepdims=True)
        filled = jnp.where(total > (iota((HAND, 1), 0) % 2).astype(F32), 1.0, 0.0)

        def token_bias(tokens, pages):
            wide = jnp.broadcast_to(tokens[:, None, :], (pages, PAGE_TOKENS, 128))
            step = iota((pages, PAGE_TOKENS, 128), 1).astype(F32)
            bias = jnp.where(step < wide, 0.0, -BIG)
            return bias.reshape(pages * PAGE_TOKENS, 128).astype(BF16)

        hand = of_page[:HAND]
        hand_bias_ref[...] = token_bias(hand * filled, HAND)
        bias_ref[0:HAND_TOKENS] = token_bias(hand * (1.0 - filled), HAND)
        bias_ref[HAND_TOKENS:TOKENS] = token_bias(of_page[HAND:], PAGES - HAND)
        new_key, new_row = iota((ROWS, 128), 0), iota((ROWS, 128), 1)
        seen = (new_key // STEPS == new_row // STEPS) & (new_key <= new_row)
        bias_ref[TOKENS : TOKENS + ROWS] = jnp.where(seen, 0.0, -BIG).astype(BF16)
        bias_ref[TOKENS + ROWS :] = jnp.full((CHUNK - ROWS, 128), -BIG, BF16)
        k_ref[TOKENS : TOKENS + ROWS] = new_k_ref[...]
        v_ref[TOKENS : TOKENS + ROWS] = new_v_ref[...]
        k_ref[TOKENS + ROWS :] = jnp.zeros((CHUNK - ROWS, WIDTH), BF16)
        v_ref[TOKENS + ROWS :] = jnp.zeros((CHUNK - ROWS, WIDTH), BF16)
        lane = iota((8, ROWS), 1)
        targets = []
        owners = [own_ref[i] for i in range(PPD * TOP)]
        for t in range(TOP):
            target = jnp.zeros((8, ROWS), I32)
            for p in range(PPD):
                i = p * TOP + t
                rank = jnp.int32(0)
                for e in range(i):
                    rank = rank + jnp.where(owners[e] == owners[i], 1, 0)
                target = jnp.where(lane // PAGE_TOKENS == p, owners[i] * 2 + rank, target)
            targets.append(target[0:1])
        slot = iota((HAND_TOKENS, ROWS), 0)
        column = iota((HAND_TOKENS, ROWS), 1)
        to_slot = (slot // PAGE_TOKENS == targets[0]) | (slot // PAGE_TOKENS == targets[1])
        same = slot % PAGE_TOKENS == column % PAGE_TOKENS
        pick_ref[...] = jnp.where(to_slot & same, 1.0, 0.0).astype(BF16)
        for copy in copies:
            copy.wait()

        def rows(c):
            return pl.ds(pl.multiple_of(c * CHUNK, CHUNK), CHUNK)

        def one_head(j, carry):
            attend(
                j, qa_ref, POOL_CHUNKS,
                lambda c, j: k_ref[rows(c), head_lanes(j)],
                lambda c, j: v_ref[rows(c), head_lanes(j)],
                lambda c: bias_ref[rows(c)],
                s_ref, mx_ref, m_ref, acc_ref, True,
            )
            return carry

        lax.fori_loop(0, KV_HEADS, one_head, 0)


def pool_attend(info, own, lengths, table, owners, q, new_k, new_v, cache_k, cache_v):
    total = POOL_CHUNKS * CHUNK
    smem = pl.BlockSpec(memory_space=pltpu.SMEM)
    hbm = pl.BlockSpec(memory_space=pl.ANY)
    return pl.pallas_call(
        pool_kernel,
        out_shape=STATE
        + [
            jax.ShapeDtypeStruct((KV_HEADS, QROWS, 2 * HEAD_WIDTH), BF16),
            jax.ShapeDtypeStruct((HAND_TOKENS, 128), BF16),
            jax.ShapeDtypeStruct((HAND_TOKENS, ROWS), BF16),
        ],
        in_specs=[smem, smem, smem] + [vmem()] * 5 + [hbm, hbm],
        out_specs=[vmem()] * 5,
        scratch_shapes=[
            pltpu.VMEM((total, WIDTH), BF16),
            pltpu.VMEM((total, WIDTH), BF16),
            pltpu.VMEM((total, 128), BF16),
            pltpu.VMEM((POOL_CHUNKS, QROWS, CHUNK), F32),
            pltpu.VMEM((QROWS, 128), F32),
            pltpu.SemaphoreType.DMA((2, 4)),
        ],
        compiler_params=pltpu.CompilerParams(vmem_limit_bytes=VMEM_LIMIT),
        cost_estimate=pl.CostEstimate(
            flops=4 * KV_HEADS * QROWS * total * 256,
            bytes_accessed=total * WIDTH * 4,
            transcendentals=KV_HEADS * QROWS * total,
        ),
    )(info, own, lengths, table, owners, q, new_k, new_v, cache_k, cache_v)


def pick_kernel(pick_ref, kv_ref, out_ref):
    for i in range(2):
        rows = jnp.dot(pick_ref[...], kv_ref[i], preferred_element_type=F32).astype(BF16)
        out_ref[:, i] = rows.reshape(HAND // 2, 2 * PAGE_TOKENS, WIDTH)


def pick_pages(pick, kv):
    return pl.pallas_call(
        pick_kernel,
        out_shape=jax.ShapeDtypeStruct((HAND // 2, 2, 2 * PAGE_TOKENS, WIDTH), BF16),
        in_specs=[vmem(), vmem()],
        out_specs=vmem(),
        compiler_params=pltpu.CompilerParams(vmem_limit_bytes=VMEM_LIMIT),
    )(pick, kv)


def hand_kernel(arrived_ref, bias_ref, qa_ref, m_in, acc_in, out_ref, s_ref, mx_ref, m_ref, acc_ref):
    m_ref[...] = m_in[...]
    acc_ref[...] = acc_in[...]
    part = CHUNK // (2 * PAGE_TOKENS)

    def chunk(c, i, j):
        at = pl.ds(c * part, part)
        return arrived_ref[at, i, :, head_lanes(j)].reshape(CHUNK, HEAD_WIDTH)

    def one_head(j, carry):
        attend(
            j, qa_ref, HAND_TOKENS // CHUNK,
            lambda c, j: chunk(c, 0, j),
            lambda c, j: chunk(c, 1, j),
            lambda c: bias_ref[pl.ds(pl.multiple_of(c * CHUNK, CHUNK), CHUNK)],
            s_ref, mx_ref, m_ref, acc_ref, False,
        )
        return carry

    lax.fori_loop(0, KV_HEADS, one_head, 0)
    finish(acc_ref, out_ref)


def hand_attend(arrived, bias, qa, m, acc):
    return pl.pallas_call(
        hand_kernel,
        out_shape=jax.ShapeDtypeStruct((ROWS, KV_HEADS * GROUP_WIDTH * HEAD_WIDTH), BF16),
        in_specs=[vmem()] * 5,
        out_specs=vmem(),
        scratch_shapes=[
            pltpu.VMEM((HAND_TOKENS // CHUNK, QROWS, CHUNK), F32),
            pltpu.VMEM((QROWS, 128), F32),
        ]
        + [pltpu.VMEM(s.shape, s.dtype) for s in STATE],
        compiler_params=pltpu.CompilerParams(vmem_limit_bytes=VMEM_LIMIT),
    )(arrived, bias, qa, m, acc)


def body(
    queries, keys, values, page_owner, lengths, page_table, group_cache_keys, group_cache_values
):
    section = lax.axis_index("s")
    x, y, c = place()
    info = jnp.stack([x, y, c, section]).astype(I32)
    me = (x * 4 + y) * 2 + c
    q = queries[0]
    kv = jnp.stack([keys[0], values[0]])

    def first_hop(k):
        def target(x, y, c, s):
            if s == 1:
                return None
            return (x, y + k, c, s) if c == 0 else (x + k, y, c, s)

        return moved(kv, ("x", "y", "c", "s"), target)

    near = [first_hop(k) for k in (1, 2, 3)]
    crossed = moved(kv, ("s",), lambda s: (1,) if s == 0 else None)
    own = lax.dynamic_slice_in_dim(page_owner.reshape(-1), me * PPD * TOP, PPD * TOP)
    m, acc, qa, hand_bias, pick = pool_attend(
        info, own, lengths, page_table, page_owner.reshape(1, PAGES), q, keys[0], values[0],
        group_cache_keys.reshape(TOKENS, WIDTH), group_cache_values.reshape(TOKENS, WIDTH),
    )

    def prompt(q, kv, near, crossed, *_):
        block = jnp.stack([kv] + near)

        def second_hop(k):
            def target(x, y, c):
                return (x + k, y, c) if c == 0 else (x, y + k, c)

            return moved(block, CTX, target)

        def other_core(piece):
            return moved(piece, ("c",), lambda c: (1 - c,))

        block_other = other_core(block)
        far = [second_hop(k) for k in (1, 2, 3)]
        state = prompt_attend(info, q, [block, block_other], [(False, 0), (True, 0)], None, False)
        far_other = [other_core(piece) for piece in far]
        state = prompt_attend(info, q, far, [(False, k) for k in (1, 2, 3)], state, False)
        return prompt_attend(info, q, far_other, [(True, k) for k in (1, 2, 3)], state, True)

    def decode(q, kv, near, crossed, m, acc, qa, hand_bias, pick):
        outgoing = pick_pages(pick, crossed)
        arrived = lax.all_to_all(outgoing, CTX, 0, 0, tiled=True)
        return hand_attend(arrived, hand_bias, qa, m, acc)

    out = lax.cond(
        section == 0, prompt, decode, q, kv, near, crossed, m, acc, qa, hand_bias, pick
    )
    return out[None]


def solution(mesh):
    inner = Mesh(mesh.devices.reshape([SIZES[a] for a in AXES]), AXES)
    return jax.shard_map(
        body,
        mesh=inner,
        in_specs=(
            P("s", CTX, "t"),
            P("s", CTX, "t"),
            P("s", CTX, "t"),
            P(),
            P(CTX, None),
            P(CTX, None),
            P(CTX, None, "t"),
            P(CTX, None, "t"),
        ),
        out_specs=P("s", CTX, "t"),
        check_vma=False,
    )
```

```python
import math

import jax
import jax.numpy as jnp
import numpy as np
from jax import lax
from jax.experimental import pallas as pl
from jax.experimental.pallas import tpu as pltpu
from jax.sharding import Mesh
from jax.sharding import PartitionSpec as P

HEAD_WIDTH = 128
GROUP_WIDTH = 8
KV_HEADS = 2
ROWS = 64
QROWS = GROUP_WIDTH * ROWS
WIDTH = KV_HEADS * HEAD_WIDTH
QUERY_WIDTH = GROUP_WIDTH * WIDTH
PAGE_TOKENS = 8
PAGES = 512
HAND = 64
SEQS = 16
STEPS = 4
TOP = 2
PPD = 8
PROMPT_PAGES = 256
TOKENS = PAGES * PAGE_TOKENS
HAND_TOKENS = HAND * PAGE_TOKENS
CHUNK = 512
NEW = 128
BIG = float(2**20)
TO_LOG2 = HEAD_WIDTH**-0.5 * math.log2(math.e)
SIDE = 4
AXES = ("x", "y", "c", "t", "s")
SIZES = {"x": 4, "y": 4, "c": 2, "t": 4, "s": 2}
CTX = ("x", "y", "c")
VMEM_LIMIT = 40 * 1024 * 1024
F32 = jnp.float32
BF16 = jnp.bfloat16
I32 = jnp.int32
HBM = pl.BlockSpec(memory_space=pltpu.HBM)
VMEM = pl.BlockSpec(memory_space=pltpu.VMEM)
STATE = [
    jax.ShapeDtypeStruct((KV_HEADS, QROWS, 128), F32),
    jax.ShapeDtypeStruct((KV_HEADS, QROWS, 2 * HEAD_WIDTH), F32),
]
ASKED = jax.ShapeDtypeStruct((KV_HEADS, QROWS, 2 * HEAD_WIDTH), BF16)
ANSWER = jax.ShapeDtypeStruct((ROWS, QUERY_WIDTH), BF16)


def moved(shard, axes, target):
    sizes = [SIZES[a] for a in axes]
    pairs = []
    for source in range(math.prod(sizes)):
        place = [int(i) for i in np.unravel_index(source, sizes)]
        goal = target(*place)
        if goal is not None:
            goal = [a % b for a, b in zip(goal, sizes)]
            pairs.append((source, int(np.ravel_multi_index(goal, sizes))))
    return lax.ppermute(shard, axes if len(axes) > 1 else axes[0], pairs)


def cost(keys):
    return pl.CostEstimate(
        flops=4 * KV_HEADS * QROWS * keys * 256,
        bytes_accessed=keys * WIDTH * 4,
        transcendentals=KV_HEADS * QROWS * keys,
    )


def iota(shape, axis):
    return lax.broadcasted_iota(I32, shape, axis)


def lanes(j):
    return pl.ds(pl.multiple_of(j * HEAD_WIDTH, HEAD_WIDTH), HEAD_WIDTH)


def ask(q_hbm, qa_ref, sem):
    copies = []
    for h in range(KV_HEADS * GROUP_WIDTH):
        source = q_hbm.at[:, pl.ds(h * HEAD_WIDTH, HEAD_WIDTH)]
        j, g = divmod(h, GROUP_WIDTH)
        goal = qa_ref.at[j, pl.ds(g * ROWS, ROWS), pl.ds(0, HEAD_WIDTH)]
        copies.append(pltpu.make_async_copy(source, goal, sem.at[h]))
    return copies


def mark_rows(qa_ref):
    hot = jnp.where(iota((QROWS, 128), 0) % ROWS == iota((QROWS, 128), 1), 1.0, 0.0).astype(BF16)
    for j in range(KV_HEADS):
        qa_ref[j, :, HEAD_WIDTH:] = hot


def score(q, keys, bias):
    wide = jnp.concatenate([keys, bias], axis=1)
    return lax.dot_general(q, wide, (((1,), (1,)), ((), ())), preferred_element_type=F32)


def peak(s):
    parts = [s[:, i : i + 128] for i in range(0, s.shape[1], 128)]
    while len(parts) > 1:
        pairs = [jnp.maximum(a, b) for a, b in zip(parts[::2], parts[1::2])]
        parts = pairs + parts[len(parts) // 2 * 2 :]
    return parts[0]


def spread(column):
    return jnp.broadcast_to(jnp.max(column, axis=1, keepdims=True), (QROWS, 128))


def mix(s, low, values):
    lows = jnp.concatenate([low] * (s.shape[1] // 128), axis=1)
    weights = jnp.exp2(s * TO_LOG2 - lows).astype(BF16)
    wide = jnp.concatenate([values, jnp.ones((values.shape[0], HEAD_WIDTH), BF16)], axis=1)
    return jnp.dot(weights, wide, preferred_element_type=F32)


def attend(j, qa_ref, keys, values, bias, s_ref, m_in, acc_in):
    s = score(qa_ref[j], keys, bias)
    s_ref[j] = s
    column = peak(s)
    if m_in is not None:
        column = jnp.maximum(column, m_in[j])
    top = spread(column)
    low = top * TO_LOG2
    total = mix(s_ref[j], low, values)
    if m_in is not None:
        shrink = jnp.exp2(m_in[j] * TO_LOG2 - low)
        total = total + acc_in[j] * jnp.concatenate([shrink, shrink], axis=1)
    return top, total


def answer(j, total, answer_ref, out_hbm, sems):
    result = (total[:, :HEAD_WIDTH] / total[:, HEAD_WIDTH:]).astype(BF16)
    for g in range(GROUP_WIDTH):
        at = (j * GROUP_WIDTH + g) * HEAD_WIDTH
        answer_ref[:, at : at + HEAD_WIDTH] = result[g * ROWS : (g + 1) * ROWS]
    part = pl.ds(j * GROUP_WIDTH * HEAD_WIDTH, GROUP_WIDTH * HEAD_WIDTH)
    copy = pltpu.make_async_copy(answer_ref.at[:, part], out_hbm.at[:, part], sems.at[j])
    copy.start()
    return copy


ANSWER_SCRATCH = [pltpu.VMEM(ANSWER.shape, BF16), pltpu.SemaphoreType.DMA((KV_HEADS,))]


def prompt_kernel(pieces, first, last, *refs):
    count = len(pieces)
    keys_in_all = count * SIDE * ROWS
    if first:
        q_hbm, *refs = refs
    else:
        qa_ref, m_in, acc_in, *refs = refs
    piece_refs, refs = refs[:count], refs[count:]
    if last:
        out_hbm, *refs = refs
    else:
        m_ref, acc_ref, *refs = refs
    if first:
        qa_ref, *refs = refs
    bias_ref, s_ref, *refs = refs
    if first:
        copies = ask(q_hbm, qa_ref, refs[0])
        for copy in copies:
            copy.start()
        mark_rows(qa_ref)
    x, y, c = lax.axis_index("x"), lax.axis_index("y"), lax.axis_index("c")
    me = x * 8 + y * 2 + c
    row_pos = me * ROWS + iota((ROWS, 128), 1)
    for i, (swapped, k2) in enumerate(pieces):
        core = (1 - c) if swapped else c
        for k1 in range(SIDE):
            on_x = jnp.where(core == 0, k2, k1)
            on_y = jnp.where(core == 0, k1, k2)
            block = ((x - on_x) & 3) * 8 + ((y - on_y) & 3) * 2 + core
            key_pos = block * ROWS + iota((ROWS, 128), 0)
            bias = jnp.where(key_pos > row_pos, -BIG, 0.0).astype(BF16)
            at = (i * SIDE + k1) * ROWS
            bias_ref[at : at + ROWS, :] = bias
    if first:
        for copy in copies:
            copy.wait()

    def piece_rows(half, j):
        head = slice(j * HEAD_WIDTH, (j + 1) * HEAD_WIDTH)
        rows = slice(half * ROWS, (half + 1) * ROWS)
        parts = [ref[:, rows, head].reshape(SIDE * ROWS, HEAD_WIDTH) for ref in piece_refs]
        return jnp.concatenate(parts, axis=0)

    sent = []
    for j in range(KV_HEADS):
        top, total = attend(
            j, qa_ref, piece_rows(0, j), piece_rows(1, j), bias_ref[...], s_ref,
            None if first else m_in, None if first else acc_in,
        )
        if last:
            sent.append(answer(j, total, refs[0], out_hbm, refs[1]))
        else:
            m_ref[j] = top
            acc_ref[j] = total
    for copy in sent:
        copy.wait()


def prompt_attend(arrays, pieces, q=None, state=None, last=False):
    first = state is None
    keys = len(pieces) * SIDE * ROWS
    scratch = [pltpu.VMEM((keys, 128), BF16), pltpu.VMEM((KV_HEADS, QROWS, keys), F32)]
    if first:
        scratch.append(pltpu.SemaphoreType.DMA((KV_HEADS * GROUP_WIDTH,)))
    if last:
        scratch += ANSWER_SCRATCH

    def kernel(*refs):
        prompt_kernel(pieces, first, last, *refs)

    before = [q] if first else list(state)
    return pl.pallas_call(
        kernel,
        out_shape=ANSWER if last else STATE + [ASKED] * first,
        in_specs=([HBM] if first else [VMEM] * 3) + [VMEM] * len(pieces),
        out_specs=HBM if last else [VMEM] * (2 + first),
        scratch_shapes=scratch,
        compiler_params=pltpu.CompilerParams(vmem_limit_bytes=VMEM_LIMIT),
        cost_estimate=cost(keys),
    )(*before, *arrays)


def pool_kernel(
    len_hbm, table_hbm, owner_hbm, q_hbm, new_k_hbm, new_v_hbm, k_hbm, v_hbm,
    m_ref, acc_ref, qa_ref, hand_bias_ref, pick_ref,
    k_ref, v_ref, new_k_ref, new_v_ref, bias_ref, new_bias_ref, s_ref, new_s_ref, mx_ref,
    len_ref, table_ref, owner_ref, own_ref, sems, ask_sems,
):
    @pl.when(lax.axis_index("s") == 1)
    def _():
        small = [
            pltpu.make_async_copy(len_hbm, len_ref, sems.at[0]),
            pltpu.make_async_copy(table_hbm, table_ref, sems.at[1]),
            pltpu.make_async_copy(owner_hbm, owner_ref, sems.at[2]),
            pltpu.make_async_copy(owner_hbm, own_ref, sems.at[3]),
        ]
        large = ask(q_hbm, qa_ref, ask_sems) + [
            pltpu.make_async_copy(new_k_hbm, new_k_ref.at[pl.ds(0, ROWS)], sems.at[4]),
            pltpu.make_async_copy(new_v_hbm, new_v_ref.at[pl.ds(0, ROWS)], sems.at[5]),
            pltpu.make_async_copy(k_hbm, k_ref, sems.at[6]),
            pltpu.make_async_copy(v_hbm, v_ref, sems.at[7]),
        ]
        for copy in small + large:
            copy.start()
        me = lax.axis_index("x") * 8 + lax.axis_index("y") * 2 + lax.axis_index("c")
        mark_rows(qa_ref)
        new_key, new_row = iota((NEW, 128), 0), iota((NEW, 128), 1)
        seen = (new_key // STEPS == new_row // STEPS) & (new_key <= new_row)
        new_bias_ref[...] = jnp.where(seen & (new_key < ROWS), 0.0, -BIG).astype(BF16)
        new_k_ref[ROWS:] = jnp.zeros((NEW - ROWS, WIDTH), BF16)
        new_v_ref[ROWS:] = jnp.zeros((NEW - ROWS, WIDTH), BF16)
        for copy in small:
            copy.wait()
        sequence = iota((8, 128), 1) // STEPS
        length = jnp.zeros((8, 128), I32)
        start = jnp.zeros((8, 128), I32)
        offset = jnp.int32(0)
        for s in range(SEQS):
            one = len_ref[0, s]
            length = jnp.where(sequence == s, one, length)
            start = jnp.where(sequence == s, offset, start)
            offset = offset + ((one + PAGE_TOKENS - 1) >> 3)
        length, start = length[0:1], start[0:1]
        past = iota((PAGES, 128), 0) - start
        live = jnp.where(past >= 0, jnp.clip(length - past * PAGE_TOKENS, 0, PAGE_TOKENS), 0)
        hot = jnp.where(iota((PAGES, PAGES), 0) == table_ref[...], 1.0, 0.0).astype(BF16)
        of_page = jnp.dot(hot, live.astype(F32).astype(BF16), preferred_element_type=F32)
        page = iota((HAND, PROMPT_PAGES), 0)
        same_index = iota((HAND, PROMPT_PAGES), 1) // PPD == page // 2
        named = jnp.zeros((HAND, PROMPT_PAGES), F32)
        for t in range(TOP):
            named = named + jnp.where((owner_ref[t : t + 1] == me) & same_index, 1.0, 0.0)
        total = jnp.sum(named, axis=1, keepdims=True)
        filled = jnp.where(total > (iota((HAND, 1), 0) % 2).astype(F32), 1.0, 0.0)

        def token_bias(tokens, pages):
            wide = jnp.broadcast_to(tokens[:, None, :], (pages, PAGE_TOKENS, 128))
            step = iota((pages, PAGE_TOKENS, 128), 1).astype(F32)
            bias = jnp.where(step < wide, 0.0, -BIG)
            return bias.reshape(pages * PAGE_TOKENS, 128).astype(BF16)

        hand = of_page[:HAND]
        hand_bias_ref[...] = token_bias(hand * filled, HAND)
        bias_ref[0:HAND_TOKENS] = token_bias(hand * (1.0 - filled), HAND)
        bias_ref[HAND_TOKENS:TOKENS] = token_bias(of_page[HAND:], PAGES - HAND)
        lane = iota((8, ROWS), 1)
        owners = [own_ref[i % TOP, me * PPD + i // TOP] for i in range(PPD * TOP)]
        targets = []
        for t in range(TOP):
            target = jnp.zeros((8, ROWS), I32)
            for p in range(PPD):
                i = p * TOP + t
                rank = jnp.int32(0)
                for e in range(i):
                    rank = rank + jnp.where(owners[e] == owners[i], 1, 0)
                target = jnp.where(lane // PAGE_TOKENS == p, owners[i] * 2 + rank, target)
            targets.append(target[0:1])
        slot = iota((HAND_TOKENS, ROWS), 0)
        column = iota((HAND_TOKENS, ROWS), 1)
        to_slot = (slot // PAGE_TOKENS == targets[0]) | (slot // PAGE_TOKENS == targets[1])
        same = slot % PAGE_TOKENS == column % PAGE_TOKENS
        pick_ref[...] = jnp.where(to_slot & same, 1.0, 0.0).astype(BF16)
        for copy in large:
            copy.wait()

        def rows(c):
            return pl.ds(pl.multiple_of(c * CHUNK, CHUNK), CHUNK)

        def one_head(j, carry):
            s = score(qa_ref[j], new_k_ref[:, lanes(j)], new_bias_ref[...])
            new_s_ref[...] = s
            mx_ref[...] = s

            def scores(c, carry):
                s = score(qa_ref[j], k_ref[rows(c), lanes(j)], bias_ref[rows(c)])
                s_ref[c] = s
                mx_ref[...] = jnp.maximum(mx_ref[...], peak(s))
                return carry

            lax.fori_loop(0, TOKENS // CHUNK, scores, 0, unroll=4)
            top = spread(mx_ref[...])
            m_ref[j] = top
            mx_ref[...] = top * TO_LOG2
            acc_ref[j] = mix(new_s_ref[...], mx_ref[...], new_v_ref[:, lanes(j)])

            def mixes(c, carry):
                acc_ref[j] += mix(s_ref[c], mx_ref[...], v_ref[rows(c), lanes(j)])
                return carry

            lax.fori_loop(0, TOKENS // CHUNK, mixes, 0, unroll=4)
            return carry

        lax.fori_loop(0, KV_HEADS, one_head, 0)


def pool_attend(lengths, table, owners, q, new_k, new_v, cache_k, cache_v):
    return pl.pallas_call(
        pool_kernel,
        out_shape=STATE
        + [
            ASKED,
            jax.ShapeDtypeStruct((HAND_TOKENS, 128), BF16),
            jax.ShapeDtypeStruct((HAND_TOKENS, ROWS), BF16),
        ],
        in_specs=[HBM] * 8,
        out_specs=[VMEM] * 5,
        scratch_shapes=[
            pltpu.VMEM((TOKENS, WIDTH), BF16),
            pltpu.VMEM((TOKENS, WIDTH), BF16),
            pltpu.VMEM((NEW, WIDTH), BF16),
            pltpu.VMEM((NEW, WIDTH), BF16),
            pltpu.VMEM((TOKENS, 128), BF16),
            pltpu.VMEM((NEW, 128), BF16),
            pltpu.VMEM((TOKENS // CHUNK, QROWS, CHUNK), F32),
            pltpu.VMEM((QROWS, NEW), F32),
            pltpu.VMEM((QROWS, 128), F32),
            pltpu.SMEM((1, SEQS), I32),
            pltpu.VMEM((1, PAGES), I32),
            pltpu.VMEM((TOP, PROMPT_PAGES), I32),
            pltpu.SMEM((TOP, PROMPT_PAGES), I32),
            pltpu.SemaphoreType.DMA((8,)),
            pltpu.SemaphoreType.DMA((KV_HEADS * GROUP_WIDTH,)),
        ],
        compiler_params=pltpu.CompilerParams(vmem_limit_bytes=VMEM_LIMIT),
        cost_estimate=cost(TOKENS + NEW),
    )(lengths, table, owners, q, new_k, new_v, cache_k, cache_v)


def pick_kernel(pick_ref, kv_ref, out_ref):
    for i in range(2):
        part = kv_ref[i * ROWS : (i + 1) * ROWS]
        rows = jnp.dot(pick_ref[...], part, preferred_element_type=F32).astype(BF16)
        out_ref[:, i] = rows.reshape(HAND // 2, 2 * PAGE_TOKENS, WIDTH)


def pick_pages(pick, kv):
    return pl.pallas_call(
        pick_kernel,
        out_shape=jax.ShapeDtypeStruct((HAND // 2, 2, 2 * PAGE_TOKENS, WIDTH), BF16),
        in_specs=[VMEM, VMEM],
        out_specs=VMEM,
        compiler_params=pltpu.CompilerParams(vmem_limit_bytes=VMEM_LIMIT),
    )(pick, kv)


def hand_kernel(arrived_ref, bias_ref, qa_ref, m_in, acc_in, out_hbm, s_ref, answer_ref, sems):
    sent = []
    for j in range(KV_HEADS):
        head = slice(j * HEAD_WIDTH, (j + 1) * HEAD_WIDTH)
        _, total = attend(
            j, qa_ref,
            arrived_ref[:, 0, :, head].reshape(HAND_TOKENS, HEAD_WIDTH),
            arrived_ref[:, 1, :, head].reshape(HAND_TOKENS, HEAD_WIDTH),
            bias_ref[...], s_ref, m_in, acc_in,
        )
        sent.append(answer(j, total, answer_ref, out_hbm, sems))
    for copy in sent:
        copy.wait()


def hand_attend(arrived, bias, qa, m, acc):
    return pl.pallas_call(
        hand_kernel,
        out_shape=ANSWER,
        in_specs=[VMEM] * 5,
        out_specs=HBM,
        scratch_shapes=[pltpu.VMEM((KV_HEADS, QROWS, HAND_TOKENS), F32)] + ANSWER_SCRATCH,
        compiler_params=pltpu.CompilerParams(vmem_limit_bytes=VMEM_LIMIT),
        cost_estimate=cost(HAND_TOKENS),
    )(arrived, bias, qa, m, acc)


def body(
    queries, keys, values, page_owner, lengths, page_table, group_cache_keys, group_cache_values
):
    section = lax.axis_index("s")
    q = queries[0]
    kv = jnp.concatenate([keys[0], values[0]], axis=0)

    def first_hop(k):
        def target(x, y, c, s):
            if s == 1:
                return None
            return (x, y + k, c, s) if c == 0 else (x + k, y, c, s)

        return moved(kv, ("x", "y", "c", "s"), target)

    near = [first_hop(k) for k in (1, 3, 2)]
    later_kv, near[0] = lax.optimization_barrier((kv, near[0]))
    crossed = moved(later_kv, ("s",), lambda s: (1,) if s == 0 else None)
    m, acc, qa, hand_bias, pick = pool_attend(
        lengths, page_table, page_owner.T, q, keys[0], values[0],
        group_cache_keys.reshape(TOKENS, WIDTH), group_cache_values.reshape(TOKENS, WIDTH),
    )

    def prompt(q, kv, near, crossed, *_):
        block = jnp.stack([kv, near[0], near[2], near[1]])

        def second_hop(k):
            def target(x, y, c):
                return (x + k, y, c) if c == 0 else (x, y + k, c)

            return moved(block, CTX, target)

        def other_core(piece):
            return moved(piece, ("c",), lambda c: (1 - c,))

        block_other = other_core(block)
        hops = (1, 3, 2)
        far = [second_hop(k) for k in hops]
        m, acc, qa = prompt_attend([block, block_other], [(False, 0), (True, 0)], q=q)
        far, m, acc, qa = lax.optimization_barrier((far, m, acc, qa))
        far_other = [other_core(piece) for piece in far]
        m, acc = prompt_attend(far, [(False, k) for k in hops], state=(qa, m, acc))
        return prompt_attend(
            far_other, [(True, k) for k in hops], state=(qa, m, acc), last=True
        )

    def decode(q, kv, near, crossed, m, acc, qa, hand_bias, pick):
        outgoing = pick_pages(pick, crossed)
        arrived = lax.all_to_all(outgoing, CTX, 0, 0, tiled=True)
        return hand_attend(arrived, hand_bias, qa, m, acc)

    out = lax.cond(
        section == 0, prompt, decode, q, kv, near, crossed, m, acc, qa, hand_bias, pick
    )
    return out[None]


def solution(mesh):
    inner = Mesh(mesh.devices.reshape([SIZES[a] for a in AXES]), AXES)
    return jax.shard_map(
        body,
        mesh=inner,
        in_specs=(
            P("s", CTX, "t"),
            P("s", CTX, "t"),
            P("s", CTX, "t"),
            P(),
            P(CTX, None),
            P(CTX, None),
            P(CTX, None, "t"),
            P(CTX, None, "t"),
        ),
        out_specs=P("s", CTX, "t"),
        check_vma=False,
    )
```

```python
import math

import jax
import jax.numpy as jnp
import numpy as np
from jax import lax
from jax.experimental import pallas as pl
from jax.experimental.pallas import tpu as pltpu
from jax.sharding import Mesh
from jax.sharding import PartitionSpec as P

HEAD_WIDTH = 128
GROUP_WIDTH = 8
KV_HEADS = 2
ROWS = 64
QROWS = GROUP_WIDTH * ROWS
WIDTH = KV_HEADS * HEAD_WIDTH
QUERY_WIDTH = GROUP_WIDTH * WIDTH
PAGE_TOKENS = 8
PAGES = 512
HAND = 64
SEQS = 16
STEPS = 4
TOP = 2
PPD = 8
PROMPT_PAGES = 256
TOKENS = PAGES * PAGE_TOKENS
HAND_TOKENS = HAND * PAGE_TOKENS
CHUNK = 512
NEW = 128
BIG = float(2**20)
TO_LOG2 = HEAD_WIDTH**-0.5 * math.log2(math.e)
SIDE = 4
HOPS = (1, 3, 2)
AXES = ("x", "y", "c", "t", "s")
SIZES = {"x": 4, "y": 4, "c": 2, "t": 4, "s": 2}
CTX = ("x", "y", "c")
VMEM_LIMIT = 40 * 1024 * 1024
F32 = jnp.float32
BF16 = jnp.bfloat16
I32 = jnp.int32
HBM = pl.BlockSpec(memory_space=pltpu.HBM)
VMEM = pl.BlockSpec(memory_space=pltpu.VMEM)
STATE = [
    jax.ShapeDtypeStruct((KV_HEADS, QROWS, 128), F32),
    jax.ShapeDtypeStruct((KV_HEADS, QROWS, 2 * HEAD_WIDTH), F32),
]
ASKED = jax.ShapeDtypeStruct((KV_HEADS, QROWS, 2 * HEAD_WIDTH), BF16)
PIECE = jax.ShapeDtypeStruct((2 * ROWS, WIDTH), BF16)
ANSWER = pltpu.HBM((ROWS, QUERY_WIDTH), BF16)


def moved(shard, axes, target):
    sizes = [SIZES[a] for a in axes]
    pairs = []
    for source in range(math.prod(sizes)):
        place = [int(i) for i in np.unravel_index(source, sizes)]
        goal = target(*place)
        if goal is not None:
            goal = [a % b for a, b in zip(goal, sizes)]
            pairs.append((source, int(np.ravel_multi_index(goal, sizes))))
    return lax.ppermute(shard, axes if len(axes) > 1 else axes[0], pairs)


def cost(keys):
    return pl.CostEstimate(
        flops=4 * KV_HEADS * QROWS * keys * 256,
        bytes_accessed=keys * WIDTH * 4,
        transcendentals=KV_HEADS * QROWS * keys,
    )


def in_hbm(*arrays):
    return [pltpu.with_memory_space_constraint(a, pltpu.HBM) for a in arrays]


def iota(shape, axis):
    return lax.broadcasted_iota(I32, shape, axis)


def lanes(j):
    return pl.ds(pl.multiple_of(j * HEAD_WIDTH, HEAD_WIDTH), HEAD_WIDTH)


def ask(q_hbm, qa_ref, sem):
    copies = []
    for h in range(KV_HEADS * GROUP_WIDTH):
        source = q_hbm.at[:, pl.ds(h * HEAD_WIDTH, HEAD_WIDTH)]
        j, g = divmod(h, GROUP_WIDTH)
        goal = qa_ref.at[j, pl.ds(g * ROWS, ROWS), pl.ds(0, HEAD_WIDTH)]
        copies.append(pltpu.make_async_copy(source, goal, sem.at[h]))
    return copies


def mark_rows(qa_ref):
    hot = jnp.where(iota((QROWS, 128), 0) % ROWS == iota((QROWS, 128), 1), 1.0, 0.0).astype(BF16)
    for j in range(KV_HEADS):
        qa_ref[j, :, HEAD_WIDTH:] = hot


def score(q, keys, bias):
    wide = jnp.concatenate([keys, bias], axis=1)
    return lax.dot_general(q, wide, (((1,), (1,)), ((), ())), preferred_element_type=F32)


def peak(s):
    parts = [s[:, i : i + 128] for i in range(0, s.shape[1], 128)]
    while len(parts) > 1:
        pairs = [jnp.maximum(a, b) for a, b in zip(parts[::2], parts[1::2])]
        parts = pairs + parts[len(parts) // 2 * 2 :]
    return parts[0]


def spread(column):
    return jnp.broadcast_to(jnp.max(column, axis=1, keepdims=True), (QROWS, 128))


def mix(s, low, values):
    lows = jnp.concatenate([low] * (s.shape[1] // 128), axis=1)
    weights = jnp.exp2(s * TO_LOG2 - lows).astype(BF16)
    wide = jnp.concatenate([values, jnp.ones((values.shape[0], HEAD_WIDTH), BF16)], axis=1)
    return jnp.dot(weights, wide, preferred_element_type=F32)


def attend(j, qa_ref, keys, values, bias, s_ref, m_in, acc_in):
    s = score(qa_ref[j], keys, bias)
    s_ref[j] = s
    column = peak(s)
    if m_in is not None:
        column = jnp.maximum(column, m_in[j])
    top = spread(column)
    low = top * TO_LOG2
    total = mix(s_ref[j], low, values)
    if m_in is not None:
        shrink = jnp.exp2(m_in[j] * TO_LOG2 - low)
        total = total + acc_in[j] * jnp.concatenate([shrink, shrink], axis=1)
    return top, total


def answer(j, total, answer_ref, out_hbm, sems):
    result = (total[:, :HEAD_WIDTH] / total[:, HEAD_WIDTH:]).astype(BF16)
    for g in range(GROUP_WIDTH):
        at = (j * GROUP_WIDTH + g) * HEAD_WIDTH
        answer_ref[:, at : at + HEAD_WIDTH] = result[g * ROWS : (g + 1) * ROWS]
    part = pl.ds(j * GROUP_WIDTH * HEAD_WIDTH, GROUP_WIDTH * HEAD_WIDTH)
    copy = pltpu.make_async_copy(answer_ref.at[:, part], out_hbm.at[:, part], sems.at[j])
    copy.start()
    return copy


ANSWER_SCRATCH = [pltpu.VMEM(ANSWER.shape, BF16), pltpu.SemaphoreType.DMA((KV_HEADS,))]


def prompt_kernel(pieces, first, last, *refs):
    count = len(pieces)
    keys_in_all = count * SIDE * ROWS
    if first:
        q_hbm, *refs = refs
    else:
        qa_ref, m_in, acc_in, *refs = refs
    piece_refs, refs = refs[:count], refs[count:]
    if last:
        out_hbm, *refs = refs
    else:
        m_ref, acc_ref, *refs = refs
    if first:
        qa_ref, *refs = refs
    bias_ref, s_ref, *refs = refs
    if first:
        copies = ask(q_hbm, qa_ref, refs[0])
        for copy in copies:
            copy.start()
        mark_rows(qa_ref)
    x, y, c = lax.axis_index("x"), lax.axis_index("y"), lax.axis_index("c")
    me = x * 8 + y * 2 + c
    row_pos = me * ROWS + iota((ROWS, 128), 1)
    for i, (swapped, k2) in enumerate(pieces):
        core = (1 - c) if swapped else c
        for k1 in range(SIDE):
            on_x = jnp.where(core == 0, k2, k1)
            on_y = jnp.where(core == 0, k1, k2)
            block = ((x - on_x) & 3) * 8 + ((y - on_y) & 3) * 2 + core
            key_pos = block * ROWS + iota((ROWS, 128), 0)
            bias = jnp.where(key_pos > row_pos, -BIG, 0.0).astype(BF16)
            at = (i * SIDE + k1) * ROWS
            bias_ref[at : at + ROWS, :] = bias
    if first:
        for copy in copies:
            copy.wait()

    def piece_rows(half, j):
        head = slice(j * HEAD_WIDTH, (j + 1) * HEAD_WIDTH)
        rows = slice(half * ROWS, (half + 1) * ROWS)
        parts = [ref[:, rows, head].reshape(SIDE * ROWS, HEAD_WIDTH) for ref in piece_refs]
        return jnp.concatenate(parts, axis=0)

    sent = []
    for j in range(KV_HEADS):
        top, total = attend(
            j, qa_ref, piece_rows(0, j), piece_rows(1, j), bias_ref[...], s_ref,
            None if first else m_in, None if first else acc_in,
        )
        if last:
            sent.append(answer(j, total, refs[0], out_hbm, refs[1]))
        else:
            m_ref[j] = top
            acc_ref[j] = total
    for copy in sent:
        copy.wait()


def prompt_attend(arrays, pieces, q=None, state=None, last=False):
    first = state is None
    keys = len(pieces) * SIDE * ROWS
    scratch = [pltpu.VMEM((keys, 128), BF16), pltpu.VMEM((KV_HEADS, QROWS, keys), F32)]
    if first:
        scratch.append(pltpu.SemaphoreType.DMA((KV_HEADS * GROUP_WIDTH,)))
    if last:
        scratch += ANSWER_SCRATCH

    def kernel(*refs):
        prompt_kernel(pieces, first, last, *refs)

    before = in_hbm(q) if first else list(state)
    return pl.pallas_call(
        kernel,
        out_shape=ANSWER if last else STATE + [ASKED] * first,
        in_specs=([HBM] if first else [VMEM] * 3) + [VMEM] * len(pieces),
        out_specs=HBM if last else [VMEM] * (2 + first),
        scratch_shapes=scratch,
        compiler_params=pltpu.CompilerParams(vmem_limit_bytes=VMEM_LIMIT),
        cost_estimate=cost(keys),
    )(*before, *arrays)


def join_kernel(k_hbm, v_hbm, kv_ref, sems):
    copies = [
        pltpu.make_async_copy(part, kv_ref.at[pl.ds(i * ROWS, ROWS)], sems.at[i])
        for i, part in enumerate((k_hbm, v_hbm))
    ]
    for copy in copies:
        copy.start()
    for copy in copies:
        copy.wait()


def join(keys, values):
    return pl.pallas_call(
        join_kernel,
        out_shape=PIECE,
        in_specs=[HBM] * 2,
        out_specs=VMEM,
        scratch_shapes=[pltpu.SemaphoreType.DMA((2,))],
        compiler_params=pltpu.CompilerParams(vmem_limit_bytes=VMEM_LIMIT),
    )(*in_hbm(keys, values))


def stack_kernel(*refs):
    *parts, block_ref, again_ref = refs
    for i in range(SIDE):
        block_ref[i] = parts[i][...] if parts else jnp.zeros(PIECE.shape, BF16)
    again_ref[...] = block_ref[0]


def stack(parts):
    return pl.pallas_call(
        stack_kernel,
        out_shape=[jax.ShapeDtypeStruct((SIDE, *PIECE.shape), BF16), PIECE],
        in_specs=[VMEM] * len(parts),
        out_specs=[VMEM] * 2,
        compiler_params=pltpu.CompilerParams(vmem_limit_bytes=VMEM_LIMIT),
    )(*parts)


def pool_kernel(
    len_hbm, table_hbm, owner_hbm, q_hbm, new_k_hbm, new_v_hbm, k_hbm, v_hbm,
    m_ref, acc_ref, qa_ref, hand_bias_ref, pick_ref,
    k_ref, v_ref, new_k_ref, new_v_ref, bias_ref, new_bias_ref, s_ref, new_s_ref, mx_ref,
    len_ref, table_ref, owner_ref, own_ref, sems, ask_sems,
):
    @pl.when(lax.axis_index("s") == 1)
    def _():
        small = [
            pltpu.make_async_copy(len_hbm, len_ref, sems.at[0]),
            pltpu.make_async_copy(table_hbm, table_ref, sems.at[1]),
            pltpu.make_async_copy(owner_hbm, owner_ref, sems.at[2]),
            pltpu.make_async_copy(owner_hbm, own_ref, sems.at[3]),
        ]
        large = ask(q_hbm, qa_ref, ask_sems) + [
            pltpu.make_async_copy(new_k_hbm, new_k_ref.at[pl.ds(0, ROWS)], sems.at[4]),
            pltpu.make_async_copy(new_v_hbm, new_v_ref.at[pl.ds(0, ROWS)], sems.at[5]),
            pltpu.make_async_copy(k_hbm, k_ref, sems.at[6]),
            pltpu.make_async_copy(v_hbm, v_ref, sems.at[7]),
        ]
        for copy in small + large:
            copy.start()
        me = lax.axis_index("x") * 8 + lax.axis_index("y") * 2 + lax.axis_index("c")
        mark_rows(qa_ref)
        new_key, new_row = iota((NEW, 128), 0), iota((NEW, 128), 1)
        seen = (new_key // STEPS == new_row // STEPS) & (new_key <= new_row)
        new_bias_ref[...] = jnp.where(seen & (new_key < ROWS), 0.0, -BIG).astype(BF16)
        new_k_ref[ROWS:] = jnp.zeros((NEW - ROWS, WIDTH), BF16)
        new_v_ref[ROWS:] = jnp.zeros((NEW - ROWS, WIDTH), BF16)
        for copy in small:
            copy.wait()
        sequence = iota((8, 128), 1) // STEPS
        length = jnp.zeros((8, 128), I32)
        start = jnp.zeros((8, 128), I32)
        offset = jnp.int32(0)
        for s in range(SEQS):
            one = len_ref[0, s]
            length = jnp.where(sequence == s, one, length)
            start = jnp.where(sequence == s, offset, start)
            offset = offset + ((one + PAGE_TOKENS - 1) >> 3)
        length, start = length[0:1], start[0:1]
        past = iota((PAGES, 128), 0) - start
        live = jnp.where(past >= 0, jnp.clip(length - past * PAGE_TOKENS, 0, PAGE_TOKENS), 0)
        hot = jnp.where(iota((PAGES, PAGES), 0) == table_ref[...], 1.0, 0.0).astype(BF16)
        of_page = jnp.dot(hot, live.astype(F32).astype(BF16), preferred_element_type=F32)
        page = iota((HAND, PROMPT_PAGES), 0)
        same_index = iota((HAND, PROMPT_PAGES), 1) // PPD == page // 2
        named = jnp.zeros((HAND, PROMPT_PAGES), F32)
        for t in range(TOP):
            named = named + jnp.where((owner_ref[t : t + 1] == me) & same_index, 1.0, 0.0)
        total = jnp.sum(named, axis=1, keepdims=True)
        filled = jnp.where(total > (iota((HAND, 1), 0) % 2).astype(F32), 1.0, 0.0)

        def token_bias(tokens, pages):
            wide = jnp.broadcast_to(tokens[:, None, :], (pages, PAGE_TOKENS, 128))
            step = iota((pages, PAGE_TOKENS, 128), 1).astype(F32)
            bias = jnp.where(step < wide, 0.0, -BIG)
            return bias.reshape(pages * PAGE_TOKENS, 128).astype(BF16)

        hand = of_page[:HAND]
        hand_bias_ref[...] = token_bias(hand * filled, HAND)
        bias_ref[0:HAND_TOKENS] = token_bias(hand * (1.0 - filled), HAND)
        bias_ref[HAND_TOKENS:TOKENS] = token_bias(of_page[HAND:], PAGES - HAND)
        lane = iota((8, ROWS), 1)
        owners = [own_ref[i % TOP, me * PPD + i // TOP] for i in range(PPD * TOP)]
        targets = []
        for t in range(TOP):
            target = jnp.zeros((8, ROWS), I32)
            for p in range(PPD):
                i = p * TOP + t
                rank = jnp.int32(0)
                for e in range(i):
                    rank = rank + jnp.where(owners[e] == owners[i], 1, 0)
                target = jnp.where(lane // PAGE_TOKENS == p, owners[i] * 2 + rank, target)
            targets.append(target[0:1])
        slot = iota((HAND_TOKENS, ROWS), 0)
        column = iota((HAND_TOKENS, ROWS), 1)
        to_slot = (slot // PAGE_TOKENS == targets[0]) | (slot // PAGE_TOKENS == targets[1])
        same = slot % PAGE_TOKENS == column % PAGE_TOKENS
        pick_ref[...] = jnp.where(to_slot & same, 1.0, 0.0).astype(BF16)
        for copy in large:
            copy.wait()

        def rows(c):
            return pl.ds(pl.multiple_of(c * CHUNK, CHUNK), CHUNK)

        def one_head(j, carry):
            s = score(qa_ref[j], new_k_ref[:, lanes(j)], new_bias_ref[...])
            new_s_ref[...] = s
            mx_ref[...] = s

            def scores(c, carry):
                s = score(qa_ref[j], k_ref[rows(c), lanes(j)], bias_ref[rows(c)])
                s_ref[c] = s
                mx_ref[...] = jnp.maximum(mx_ref[...], peak(s))
                return carry

            lax.fori_loop(0, TOKENS // CHUNK, scores, 0, unroll=4)
            top = spread(mx_ref[...])
            m_ref[j] = top
            mx_ref[...] = top * TO_LOG2
            acc_ref[j] = mix(new_s_ref[...], mx_ref[...], new_v_ref[:, lanes(j)])

            def mixes(c, carry):
                acc_ref[j] += mix(s_ref[c], mx_ref[...], v_ref[rows(c), lanes(j)])
                return carry

            lax.fori_loop(0, TOKENS // CHUNK, mixes, 0, unroll=4)
            return carry

        lax.fori_loop(0, KV_HEADS, one_head, 0)


def pool_attend(lengths, table, owners, q, new_k, new_v, cache_k, cache_v):
    return pl.pallas_call(
        pool_kernel,
        out_shape=STATE
        + [
            ASKED,
            jax.ShapeDtypeStruct((HAND_TOKENS, 128), BF16),
            jax.ShapeDtypeStruct((HAND_TOKENS, ROWS), BF16),
        ],
        in_specs=[HBM] * 8,
        out_specs=[VMEM] * 5,
        scratch_shapes=[
            pltpu.VMEM((TOKENS, WIDTH), BF16),
            pltpu.VMEM((TOKENS, WIDTH), BF16),
            pltpu.VMEM((NEW, WIDTH), BF16),
            pltpu.VMEM((NEW, WIDTH), BF16),
            pltpu.VMEM((TOKENS, 128), BF16),
            pltpu.VMEM((NEW, 128), BF16),
            pltpu.VMEM((TOKENS // CHUNK, QROWS, CHUNK), F32),
            pltpu.VMEM((QROWS, NEW), F32),
            pltpu.VMEM((QROWS, 128), F32),
            pltpu.SMEM((1, SEQS), I32),
            pltpu.VMEM((1, PAGES), I32),
            pltpu.VMEM((TOP, PROMPT_PAGES), I32),
            pltpu.SMEM((TOP, PROMPT_PAGES), I32),
            pltpu.SemaphoreType.DMA((8,)),
            pltpu.SemaphoreType.DMA((KV_HEADS * GROUP_WIDTH,)),
        ],
        compiler_params=pltpu.CompilerParams(vmem_limit_bytes=VMEM_LIMIT),
        cost_estimate=cost(TOKENS + NEW),
    )(*in_hbm(lengths, table, owners, q, new_k, new_v, cache_k, cache_v))


def pick_kernel(pick_ref, kv_ref, out_ref):
    for i in range(2):
        part = kv_ref[i * ROWS : (i + 1) * ROWS]
        rows = jnp.dot(pick_ref[...], part, preferred_element_type=F32).astype(BF16)
        out_ref[:, i] = rows.reshape(HAND // 2, 2 * PAGE_TOKENS, WIDTH)


def pick_pages(pick, kv):
    return pl.pallas_call(
        pick_kernel,
        out_shape=jax.ShapeDtypeStruct((HAND // 2, 2, 2 * PAGE_TOKENS, WIDTH), BF16),
        in_specs=[VMEM, VMEM],
        out_specs=VMEM,
        compiler_params=pltpu.CompilerParams(vmem_limit_bytes=VMEM_LIMIT),
    )(pick, kv)


def hand_kernel(arrived_ref, bias_ref, qa_ref, m_in, acc_in, out_hbm, s_ref, answer_ref, sems):
    sent = []
    for j in range(KV_HEADS):
        head = slice(j * HEAD_WIDTH, (j + 1) * HEAD_WIDTH)
        _, total = attend(
            j, qa_ref,
            arrived_ref[:, 0, :, head].reshape(HAND_TOKENS, HEAD_WIDTH),
            arrived_ref[:, 1, :, head].reshape(HAND_TOKENS, HEAD_WIDTH),
            bias_ref[...], s_ref, m_in, acc_in,
        )
        sent.append(answer(j, total, answer_ref, out_hbm, sems))
    for copy in sent:
        copy.wait()


def hand_attend(arrived, bias, qa, m, acc):
    return pl.pallas_call(
        hand_kernel,
        out_shape=ANSWER,
        in_specs=[VMEM] * 5,
        out_specs=HBM,
        scratch_shapes=[pltpu.VMEM((KV_HEADS, QROWS, HAND_TOKENS), F32)] + ANSWER_SCRATCH,
        compiler_params=pltpu.CompilerParams(vmem_limit_bytes=VMEM_LIMIT),
        cost_estimate=cost(HAND_TOKENS),
    )(arrived, bias, qa, m, acc)


def body(
    queries, keys, values, page_owner, lengths, page_table, group_cache_keys, group_cache_values
):
    first_section = lax.axis_index("s") == 0
    q = queries[0]

    def shifted(part, k, swap):
        def target(x, y, c):
            return (x, y + k, c) if (c == 0) != swap else (x + k, y, c)

        return moved(part, CTX, target)

    def other_core(part):
        return moved(part, ("c",), lambda c: (1 - c,))

    def gather_near(keys, values):
        kv = join(keys, values)
        near = {k: shifted(kv, k, False) for k in HOPS}
        return stack([kv] + [near[k] for k in (1, 2, 3)])

    def wait_near(keys, values):
        return stack([])

    block, kv = lax.cond(first_section, gather_near, wait_near, keys[0], values[0])
    crossed = moved(kv, ("s",), lambda s: (1,) if s == 0 else None)
    ready = pool_attend(
        lengths, page_table, page_owner.T, q, keys[0], values[0],
        group_cache_keys.reshape(TOKENS, WIDTH), group_cache_values.reshape(TOKENS, WIDTH),
    )

    def prompt(q, block, crossed, *_):
        block_other = other_core(block)
        h = HOPS
        far = [shifted(block, k, True) for k in h]
        m, acc, qa = prompt_attend([block, block_other], [(False, 0), (True, 0)], q=q)
        far_other = []
        for i in range(3):
            far[i], m, acc = lax.optimization_barrier((far[i], m, acc))
            far_other.append(other_core(far[i]))
        m, acc = prompt_attend(
            [far[0], far[1], far_other[0]], [(False, h[0]), (False, h[1]), (True, h[0])],
            state=(qa, m, acc),
        )
        return prompt_attend(
            [far[2], far_other[1], far_other[2]], [(False, h[2]), (True, h[1]), (True, h[2])],
            state=(qa, m, acc), last=True,
        )

    def decode(q, block, crossed, m, acc, qa, hand_bias, pick):
        outgoing = pick_pages(pick, crossed)
        arrived = lax.all_to_all(outgoing, CTX, 0, 0, tiled=True)
        return hand_attend(arrived, hand_bias, qa, m, acc)

    out = lax.cond(first_section, prompt, decode, q, block, crossed, *ready)
    return out[None]


def solution(mesh):
    inner = Mesh(mesh.devices.reshape([SIZES[a] for a in AXES]), AXES)
    return jax.shard_map(
        body,
        mesh=inner,
        in_specs=(
            P("s", CTX, "t"),
            P("s", CTX, "t"),
            P("s", CTX, "t"),
            P(),
            P(CTX, None),
            P(CTX, None),
            P(CTX, None, "t"),
            P(CTX, None, "t"),
        ),
        out_specs=P("s", CTX, "t"),
        check_vma=False,
    )
```

```python
import math

import jax
import jax.numpy as jnp
import numpy as np
from jax import lax
from jax.experimental import pallas as pl
from jax.experimental.pallas import tpu as pltpu
from jax.sharding import Mesh
from jax.sharding import PartitionSpec as P

HEAD_WIDTH = 128
GROUP_WIDTH = 8
KV_HEADS = 2
ROWS = 64
QROWS = GROUP_WIDTH * ROWS
WIDTH = KV_HEADS * HEAD_WIDTH
QUERY_WIDTH = GROUP_WIDTH * WIDTH
PAGE_TOKENS = 8
PAGES = 512
HAND = 64
SEQS = 16
STEPS = 4
TOP = 2
PPD = 8
PROMPT_PAGES = 256
TOKENS = PAGES * PAGE_TOKENS
HAND_TOKENS = HAND * PAGE_TOKENS
CHUNK = 512
NEW = 128
BIG = float(2**20)
TO_LOG2 = HEAD_WIDTH**-0.5 * math.log2(math.e)
SIDE = 4
HOPS = (1, 3, 2)
AXES = ("x", "y", "c", "t", "s")
SIZES = {"x": 4, "y": 4, "c": 2, "t": 4, "s": 2}
CTX = ("x", "y", "c")
VMEM_LIMIT = 16 * 1024 * 1024
POOL_LIMIT = 24 * 1024 * 1024
F32 = jnp.float32
BF16 = jnp.bfloat16
I32 = jnp.int32
HBM = pl.BlockSpec(memory_space=pltpu.HBM)
VMEM = pl.BlockSpec(memory_space=pltpu.VMEM)
STATE = [
    jax.ShapeDtypeStruct((KV_HEADS, QROWS, 128), F32),
    jax.ShapeDtypeStruct((KV_HEADS, QROWS, 2 * HEAD_WIDTH), F32),
]
ASKED = jax.ShapeDtypeStruct((KV_HEADS, QROWS, 2 * HEAD_WIDTH), BF16)
PIECE = jax.ShapeDtypeStruct((2 * ROWS, WIDTH), BF16)
ANSWER = pltpu.HBM((ROWS, QUERY_WIDTH), BF16)


def moved(shard, axes, target):
    sizes = [SIZES[a] for a in axes]
    pairs = []
    for source in range(math.prod(sizes)):
        place = [int(i) for i in np.unravel_index(source, sizes)]
        goal = target(*place)
        if goal is not None:
            goal = [a % b for a, b in zip(goal, sizes)]
            pairs.append((source, int(np.ravel_multi_index(goal, sizes))))
    return lax.ppermute(shard, axes if len(axes) > 1 else axes[0], pairs)


def cost(keys):
    return pl.CostEstimate(
        flops=4 * KV_HEADS * QROWS * keys * 256,
        bytes_accessed=keys * WIDTH * 4,
        transcendentals=KV_HEADS * QROWS * keys,
    )


def in_hbm(*arrays):
    return [pltpu.with_memory_space_constraint(a, pltpu.HBM) for a in arrays]


def iota(shape, axis):
    return lax.broadcasted_iota(I32, shape, axis)


def lanes(j):
    return pl.ds(pl.multiple_of(j * HEAD_WIDTH, HEAD_WIDTH), HEAD_WIDTH)


def ask(q_hbm, qa_ref, sem):
    copies = []
    for h in range(KV_HEADS * GROUP_WIDTH):
        source = q_hbm.at[:, pl.ds(h * HEAD_WIDTH, HEAD_WIDTH)]
        j, g = divmod(h, GROUP_WIDTH)
        goal = qa_ref.at[j, pl.ds(g * ROWS, ROWS), pl.ds(0, HEAD_WIDTH)]
        copies.append(pltpu.make_async_copy(source, goal, sem.at[h]))
    return copies


def mark_rows(qa_ref):
    hot = jnp.where(iota((QROWS, 128), 0) % ROWS == iota((QROWS, 128), 1), 1.0, 0.0).astype(BF16)
    for j in range(KV_HEADS):
        qa_ref[j, :, HEAD_WIDTH:] = hot


def score(q, keys, bias):
    wide = jnp.concatenate([keys, bias], axis=1)
    return lax.dot_general(q, wide, (((1,), (1,)), ((), ())), preferred_element_type=F32)


def peak(s):
    parts = [s[:, i : i + 128] for i in range(0, s.shape[1], 128)]
    while len(parts) > 1:
        pairs = [jnp.maximum(a, b) for a, b in zip(parts[::2], parts[1::2])]
        parts = pairs + parts[len(parts) // 2 * 2 :]
    return parts[0]


def spread(column):
    return jnp.broadcast_to(jnp.max(column, axis=1, keepdims=True), (QROWS, 128))


def mix(s, low, values):
    lows = jnp.concatenate([low] * (s.shape[1] // 128), axis=1)
    weights = jnp.exp2(s * TO_LOG2 - lows).astype(BF16)
    wide = jnp.concatenate([values, jnp.ones((values.shape[0], HEAD_WIDTH), BF16)], axis=1)
    return jnp.dot(weights, wide, preferred_element_type=F32)


def attend(j, qa_ref, keys, values, bias, s_ref, m_in, acc_in):
    s = score(qa_ref[j], keys, bias)
    s_ref[j] = s
    column = peak(s)
    if m_in is not None:
        column = jnp.maximum(column, m_in[j])
    top = spread(column)
    low = top * TO_LOG2
    total = mix(s_ref[j], low, values)
    if m_in is not None:
        shrink = jnp.exp2(m_in[j] * TO_LOG2 - low)
        total = total + acc_in[j] * jnp.concatenate([shrink, shrink], axis=1)
    return top, total


def answer(j, total, answer_ref, out_hbm, sems):
    result = (total[:, :HEAD_WIDTH] / total[:, HEAD_WIDTH:]).astype(BF16)
    for g in range(GROUP_WIDTH):
        at = (j * GROUP_WIDTH + g) * HEAD_WIDTH
        answer_ref[:, at : at + HEAD_WIDTH] = result[g * ROWS : (g + 1) * ROWS]
    part = pl.ds(j * GROUP_WIDTH * HEAD_WIDTH, GROUP_WIDTH * HEAD_WIDTH)
    copy = pltpu.make_async_copy(answer_ref.at[:, part], out_hbm.at[:, part], sems.at[j])
    copy.start()
    return copy


ANSWER_SCRATCH = [pltpu.VMEM(ANSWER.shape, BF16), pltpu.SemaphoreType.DMA((KV_HEADS,))]


def prompt_kernel(pieces, first, last, *refs):
    count = len(pieces)
    keys_in_all = count * SIDE * ROWS
    if first:
        q_hbm, *refs = refs
    else:
        qa_ref, m_in, acc_in, *refs = refs
    piece_refs, refs = refs[:count], refs[count:]
    if last:
        out_hbm, *refs = refs
    else:
        m_ref, acc_ref, *refs = refs
    if first:
        qa_ref, *refs = refs
    bias_ref, s_ref, *refs = refs
    if first:
        copies = ask(q_hbm, qa_ref, refs[0])
        for copy in copies:
            copy.start()
        mark_rows(qa_ref)
    x, y, c = lax.axis_index("x"), lax.axis_index("y"), lax.axis_index("c")
    me = x * 8 + y * 2 + c
    row_pos = me * ROWS + iota((ROWS, 128), 1)
    for i, (swapped, k2) in enumerate(pieces):
        core = (1 - c) if swapped else c
        for k1 in range(SIDE):
            on_x = jnp.where(core == 0, k2, k1)
            on_y = jnp.where(core == 0, k1, k2)
            block = ((x - on_x) & 3) * 8 + ((y - on_y) & 3) * 2 + core
            key_pos = block * ROWS + iota((ROWS, 128), 0)
            bias = jnp.where(key_pos > row_pos, -BIG, 0.0).astype(BF16)
            at = (i * SIDE + k1) * ROWS
            bias_ref[at : at + ROWS, :] = bias
    if first:
        for copy in copies:
            copy.wait()

    def piece_rows(half, j):
        head = slice(j * HEAD_WIDTH, (j + 1) * HEAD_WIDTH)
        rows = slice(half * ROWS, (half + 1) * ROWS)
        parts = [ref[:, rows, head].reshape(SIDE * ROWS, HEAD_WIDTH) for ref in piece_refs]
        return jnp.concatenate(parts, axis=0)

    sent = []
    for j in range(KV_HEADS):
        top, total = attend(
            j, qa_ref, piece_rows(0, j), piece_rows(1, j), bias_ref[...], s_ref,
            None if first else m_in, None if first else acc_in,
        )
        if last:
            sent.append(answer(j, total, refs[0], out_hbm, refs[1]))
        else:
            m_ref[j] = top
            acc_ref[j] = total
    for copy in sent:
        copy.wait()


def prompt_attend(arrays, pieces, q=None, state=None, last=False):
    first = state is None
    keys = len(pieces) * SIDE * ROWS
    scratch = [pltpu.VMEM((keys, 128), BF16), pltpu.VMEM((KV_HEADS, QROWS, keys), F32)]
    if first:
        scratch.append(pltpu.SemaphoreType.DMA((KV_HEADS * GROUP_WIDTH,)))
    if last:
        scratch += ANSWER_SCRATCH

    def kernel(*refs):
        prompt_kernel(pieces, first, last, *refs)

    before = in_hbm(q) if first else list(state)
    return pl.pallas_call(
        kernel,
        out_shape=ANSWER if last else STATE + [ASKED] * first,
        in_specs=([HBM] if first else [VMEM] * 3) + [VMEM] * len(pieces),
        out_specs=HBM if last else [VMEM] * (2 + first),
        scratch_shapes=scratch,
        compiler_params=pltpu.CompilerParams(vmem_limit_bytes=VMEM_LIMIT),
        cost_estimate=cost(keys),
    )(*before, *arrays)


def join_kernel(k_hbm, v_hbm, kv_ref, sems):
    copies = [
        pltpu.make_async_copy(part, kv_ref.at[pl.ds(i * ROWS, ROWS)], sems.at[i])
        for i, part in enumerate((k_hbm, v_hbm))
    ]
    for copy in copies:
        copy.start()
    for copy in copies:
        copy.wait()


def join(keys, values):
    return pl.pallas_call(
        join_kernel,
        out_shape=PIECE,
        in_specs=[HBM] * 2,
        out_specs=VMEM,
        scratch_shapes=[pltpu.SemaphoreType.DMA((2,))],
        compiler_params=pltpu.CompilerParams(vmem_limit_bytes=VMEM_LIMIT),
    )(*in_hbm(keys, values))


BLOCK = jax.ShapeDtypeStruct((SIDE, *PIECE.shape), BF16)


def place_kernel(count, *refs):
    parts, outs = refs[:count], refs[count:]
    slots = [out.at[i] for out in outs for i in range(out.shape[0])]
    for i, slot in enumerate(slots):
        slot[...] = parts[i][...] if parts else jnp.zeros(slot.shape, BF16)


def place(parts, counts):
    def kernel(*refs):
        place_kernel(len(parts), *refs)

    return pl.pallas_call(
        kernel,
        out_shape=[pltpu.VMEM((n, *PIECE.shape), BF16) for n in counts],
        in_specs=[VMEM] * len(parts),
        out_specs=[VMEM] * len(counts),
        compiler_params=pltpu.CompilerParams(vmem_limit_bytes=VMEM_LIMIT),
    )(*parts)


def after_kernel(part_ref, state_ref, out_ref):
    out_ref[...] = part_ref[...]


def after(part, state):
    return pl.pallas_call(
        after_kernel,
        out_shape=pltpu.VMEM(part.shape, part.dtype),
        in_specs=[VMEM, VMEM],
        out_specs=VMEM,
        compiler_params=pltpu.CompilerParams(vmem_limit_bytes=VMEM_LIMIT),
    )(part, state)


def pool_kernel(
    len_hbm, table_hbm, owner_hbm, q_hbm, new_k_hbm, new_v_hbm, k_hbm, v_hbm,
    m_ref, acc_ref, qa_ref, hand_bias_ref, pick_ref,
    k_ref, v_ref, new_k_ref, new_v_ref, bias_ref, new_bias_ref, s_ref, new_s_ref, mx_ref,
    len_ref, table_ref, owner_ref, own_ref, sems, ask_sems,
):
    @pl.when(lax.axis_index("s") == 1)
    def _():
        small = [
            pltpu.make_async_copy(len_hbm, len_ref, sems.at[0]),
            pltpu.make_async_copy(table_hbm, table_ref, sems.at[1]),
            pltpu.make_async_copy(owner_hbm, owner_ref, sems.at[2]),
            pltpu.make_async_copy(owner_hbm, own_ref, sems.at[3]),
        ]
        large = ask(q_hbm, qa_ref, ask_sems) + [
            pltpu.make_async_copy(new_k_hbm, new_k_ref.at[pl.ds(0, ROWS)], sems.at[4]),
            pltpu.make_async_copy(new_v_hbm, new_v_ref.at[pl.ds(0, ROWS)], sems.at[5]),
            pltpu.make_async_copy(k_hbm, k_ref, sems.at[6]),
            pltpu.make_async_copy(v_hbm, v_ref, sems.at[7]),
        ]
        for copy in small + large:
            copy.start()
        me = lax.axis_index("x") * 8 + lax.axis_index("y") * 2 + lax.axis_index("c")
        mark_rows(qa_ref)
        new_key, new_row = iota((NEW, 128), 0), iota((NEW, 128), 1)
        seen = (new_key // STEPS == new_row // STEPS) & (new_key <= new_row)
        new_bias_ref[...] = jnp.where(seen & (new_key < ROWS), 0.0, -BIG).astype(BF16)
        new_k_ref[ROWS:] = jnp.zeros((NEW - ROWS, WIDTH), BF16)
        new_v_ref[ROWS:] = jnp.zeros((NEW - ROWS, WIDTH), BF16)
        for copy in small:
            copy.wait()
        sequence = iota((8, 128), 1) // STEPS
        length = jnp.zeros((8, 128), I32)
        start = jnp.zeros((8, 128), I32)
        offset = jnp.int32(0)
        for s in range(SEQS):
            one = len_ref[0, s]
            length = jnp.where(sequence == s, one, length)
            start = jnp.where(sequence == s, offset, start)
            offset = offset + ((one + PAGE_TOKENS - 1) >> 3)
        length, start = length[0:1], start[0:1]
        past = iota((PAGES, 128), 0) - start
        live = jnp.where(past >= 0, jnp.clip(length - past * PAGE_TOKENS, 0, PAGE_TOKENS), 0)
        hot = jnp.where(iota((PAGES, PAGES), 0) == table_ref[...], 1.0, 0.0).astype(BF16)
        of_page = jnp.dot(hot, live.astype(F32).astype(BF16), preferred_element_type=F32)
        page = iota((HAND, PROMPT_PAGES), 0)
        same_index = iota((HAND, PROMPT_PAGES), 1) // PPD == page // 2
        named = jnp.zeros((HAND, PROMPT_PAGES), F32)
        for t in range(TOP):
            named = named + jnp.where((owner_ref[t : t + 1] == me) & same_index, 1.0, 0.0)
        total = jnp.sum(named, axis=1, keepdims=True)
        filled = jnp.where(total > (iota((HAND, 1), 0) % 2).astype(F32), 1.0, 0.0)

        def token_bias(tokens, pages):
            wide = jnp.broadcast_to(tokens[:, None, :], (pages, PAGE_TOKENS, 128))
            step = iota((pages, PAGE_TOKENS, 128), 1).astype(F32)
            bias = jnp.where(step < wide, 0.0, -BIG)
            return bias.reshape(pages * PAGE_TOKENS, 128).astype(BF16)

        hand = of_page[:HAND]
        hand_bias_ref[...] = token_bias(hand * filled, HAND)
        bias_ref[0:HAND_TOKENS] = token_bias(hand * (1.0 - filled), HAND)
        bias_ref[HAND_TOKENS:TOKENS] = token_bias(of_page[HAND:], PAGES - HAND)
        lane = iota((8, ROWS), 1)
        owners = [own_ref[i % TOP, me * PPD + i // TOP] for i in range(PPD * TOP)]
        targets = []
        for t in range(TOP):
            target = jnp.zeros((8, ROWS), I32)
            for p in range(PPD):
                i = p * TOP + t
                rank = jnp.int32(0)
                for e in range(i):
                    rank = rank + jnp.where(owners[e] == owners[i], 1, 0)
                target = jnp.where(lane // PAGE_TOKENS == p, owners[i] * 2 + rank, target)
            targets.append(target[0:1])
        slot = iota((HAND_TOKENS, ROWS), 0)
        column = iota((HAND_TOKENS, ROWS), 1)
        to_slot = (slot // PAGE_TOKENS == targets[0]) | (slot // PAGE_TOKENS == targets[1])
        same = slot % PAGE_TOKENS == column % PAGE_TOKENS
        pick_ref[...] = jnp.where(to_slot & same, 1.0, 0.0).astype(BF16)
        for copy in large:
            copy.wait()

        def rows(c):
            return pl.ds(pl.multiple_of(c * CHUNK, CHUNK), CHUNK)

        def one_head(j, carry):
            s = score(qa_ref[j], new_k_ref[:, lanes(j)], new_bias_ref[...])
            new_s_ref[...] = s
            mx_ref[...] = s

            def scores(c, carry):
                s = score(qa_ref[j], k_ref[rows(c), lanes(j)], bias_ref[rows(c)])
                s_ref[c] = s
                mx_ref[...] = jnp.maximum(mx_ref[...], peak(s))
                return carry

            lax.fori_loop(0, TOKENS // CHUNK, scores, 0, unroll=4)
            top = spread(mx_ref[...])
            m_ref[j] = top
            mx_ref[...] = top * TO_LOG2
            acc_ref[j] = mix(new_s_ref[...], mx_ref[...], new_v_ref[:, lanes(j)])

            def mixes(c, carry):
                acc_ref[j] += mix(s_ref[c], mx_ref[...], v_ref[rows(c), lanes(j)])
                return carry

            lax.fori_loop(0, TOKENS // CHUNK, mixes, 0, unroll=4)
            return carry

        lax.fori_loop(0, KV_HEADS, one_head, 0)


def pool_attend(lengths, table, owners, q, new_k, new_v, cache_k, cache_v):
    return pl.pallas_call(
        pool_kernel,
        out_shape=STATE
        + [
            ASKED,
            jax.ShapeDtypeStruct((HAND_TOKENS, 128), BF16),
            jax.ShapeDtypeStruct((HAND_TOKENS, ROWS), BF16),
        ],
        in_specs=[HBM] * 8,
        out_specs=[VMEM] * 5,
        scratch_shapes=[
            pltpu.VMEM((TOKENS, WIDTH), BF16),
            pltpu.VMEM((TOKENS, WIDTH), BF16),
            pltpu.VMEM((NEW, WIDTH), BF16),
            pltpu.VMEM((NEW, WIDTH), BF16),
            pltpu.VMEM((TOKENS, 128), BF16),
            pltpu.VMEM((NEW, 128), BF16),
            pltpu.VMEM((TOKENS // CHUNK, QROWS, CHUNK), F32),
            pltpu.VMEM((QROWS, NEW), F32),
            pltpu.VMEM((QROWS, 128), F32),
            pltpu.SMEM((1, SEQS), I32),
            pltpu.VMEM((1, PAGES), I32),
            pltpu.VMEM((TOP, PROMPT_PAGES), I32),
            pltpu.SMEM((TOP, PROMPT_PAGES), I32),
            pltpu.SemaphoreType.DMA((8,)),
            pltpu.SemaphoreType.DMA((KV_HEADS * GROUP_WIDTH,)),
        ],
        compiler_params=pltpu.CompilerParams(vmem_limit_bytes=POOL_LIMIT),
        cost_estimate=cost(TOKENS + NEW),
    )(*in_hbm(lengths, table, owners, q, new_k, new_v, cache_k, cache_v))


def pick_kernel(pick_ref, kv_ref, out_ref):
    for i in range(2):
        part = kv_ref[i * ROWS : (i + 1) * ROWS]
        rows = jnp.dot(pick_ref[...], part, preferred_element_type=F32).astype(BF16)
        out_ref[:, i] = rows.reshape(HAND // 2, 2 * PAGE_TOKENS, WIDTH)


def pick_pages(pick, kv):
    return pl.pallas_call(
        pick_kernel,
        out_shape=jax.ShapeDtypeStruct((HAND // 2, 2, 2 * PAGE_TOKENS, WIDTH), BF16),
        in_specs=[VMEM, VMEM],
        out_specs=VMEM,
        compiler_params=pltpu.CompilerParams(vmem_limit_bytes=VMEM_LIMIT),
    )(pick, kv)


def hand_kernel(arrived_ref, bias_ref, qa_ref, m_in, acc_in, out_hbm, s_ref, answer_ref, sems):
    sent = []
    for j in range(KV_HEADS):
        head = slice(j * HEAD_WIDTH, (j + 1) * HEAD_WIDTH)
        _, total = attend(
            j, qa_ref,
            arrived_ref[:, 0, :, head].reshape(HAND_TOKENS, HEAD_WIDTH),
            arrived_ref[:, 1, :, head].reshape(HAND_TOKENS, HEAD_WIDTH),
            bias_ref[...], s_ref, m_in, acc_in,
        )
        sent.append(answer(j, total, answer_ref, out_hbm, sems))
    for copy in sent:
        copy.wait()


def hand_attend(arrived, bias, qa, m, acc):
    return pl.pallas_call(
        hand_kernel,
        out_shape=ANSWER,
        in_specs=[VMEM] * 5,
        out_specs=HBM,
        scratch_shapes=[pltpu.VMEM((KV_HEADS, QROWS, HAND_TOKENS), F32)] + ANSWER_SCRATCH,
        compiler_params=pltpu.CompilerParams(vmem_limit_bytes=VMEM_LIMIT),
        cost_estimate=cost(HAND_TOKENS),
    )(arrived, bias, qa, m, acc)


def body(
    queries, keys, values, page_owner, lengths, page_table, group_cache_keys, group_cache_values
):
    first_section = lax.axis_index("s") == 0
    q = queries[0]

    def shifted(part, k, swap):
        def target(x, y, c):
            return (x, y + k, c) if (c == 0) != swap else (x + k, y, c)

        return moved(part, CTX, target)

    def other_core(part):
        return moved(part, ("c",), lambda c: (1 - c,))

    def next_ones(keys, values):
        kv = join(keys, values)
        return tuple(place([kv, kv, shifted(kv, 1, False), shifted(kv, 3, False)], [1, 3]))

    kv, three = lax.cond(
        first_section, next_ones, lambda *_: tuple(place([], [1, 3])), keys[0], values[0]
    )
    crossed = moved(kv[0], ("s",), lambda s: (1,) if s == 0 else None)

    def the_last(three):
        kv, near, back = three[0], three[1], three[2]
        return place([kv, near, shifted(kv, 2, False), back], [SIDE])[0]

    block = lax.cond(first_section, the_last, lambda *_: place([], [SIDE])[0], three)
    ready = pool_attend(
        lengths, page_table, page_owner.T, q, keys[0], values[0],
        group_cache_keys.reshape(TOKENS, WIDTH), group_cache_values.reshape(TOKENS, WIDTH),
    )

    def prompt(q, block, crossed, *_):
        block_other = other_core(block)
        h = HOPS
        far = [shifted(block, k, True) for k in h]
        m, acc, qa = prompt_attend([block, block_other], [(False, 0), (True, 0)], q=q)
        far_other = []
        for i in range(2):
            far[i], m, acc = lax.optimization_barrier((far[i], m, acc))
            far_other.append(other_core(far[i]))
        m, acc = prompt_attend(
            [far[0], far[1], far_other[0]], [(False, h[0]), (False, h[1]), (True, h[0])],
            state=(qa, m, acc),
        )
        last = far[2]
        far_other.append(other_core(last))
        m, acc = prompt_attend(
            [far_other[1], last], [(True, h[1]), (False, h[2])], state=(qa, m, acc)
        )
        return prompt_attend([far_other[2]], [(True, h[2])], state=(qa, m, acc), last=True)

    def decode(q, block, crossed, m, acc, qa, hand_bias, pick):
        outgoing = pick_pages(pick, crossed)
        arrived = lax.all_to_all(outgoing, CTX, 0, 0, tiled=True)
        return hand_attend(arrived, hand_bias, qa, m, acc)

    out = lax.cond(first_section, prompt, decode, q, block, crossed, *ready)
    return out[None]


def solution(mesh):
    inner = Mesh(mesh.devices.reshape([SIZES[a] for a in AXES]), AXES)
    return jax.shard_map(
        body,
        mesh=inner,
        in_specs=(
            P("s", CTX, "t"),
            P("s", CTX, "t"),
            P("s", CTX, "t"),
            P(),
            P(CTX, None),
            P(CTX, None),
            P(CTX, None, "t"),
            P(CTX, None, "t"),
        ),
        out_specs=P("s", CTX, "t"),
        check_vma=False,
    )
```

```python
import math

import jax
import jax.numpy as jnp
import numpy as np
from jax import lax
from jax.experimental import pallas as pl
from jax.experimental.pallas import tpu as pltpu
from jax.sharding import Mesh
from jax.sharding import PartitionSpec as P

HEAD_WIDTH = 128
GROUP_WIDTH = 8
KV_HEADS = 2
ROWS = 64
QROWS = GROUP_WIDTH * ROWS
WIDTH = KV_HEADS * HEAD_WIDTH
QUERY_WIDTH = GROUP_WIDTH * WIDTH
PAGE_TOKENS = 8
PAGES = 512
HAND = 64
SEQS = 16
STEPS = 4
TOP = 2
PPD = 8
PROMPT_PAGES = 256
TOKENS = PAGES * PAGE_TOKENS
HAND_TOKENS = HAND * PAGE_TOKENS
CHUNK = 512
HALF_CHUNKS = TOKENS // CHUNK // 2
NEW = 128
BIG = float(2**20)
TO_LOG2 = HEAD_WIDTH**-0.5 * math.log2(math.e)
SIDE = 4
HOPS = (1, 3, 2)
AXES = ("x", "y", "c", "t", "s")
SIZES = {"x": 4, "y": 4, "c": 2, "t": 4, "s": 2}
CTX = ("x", "y", "c")
VMEM_LIMIT = 16 * 1024 * 1024
POOL_LIMIT = 24 * 1024 * 1024
F32 = jnp.float32
BF16 = jnp.bfloat16
I32 = jnp.int32
HBM = pl.BlockSpec(memory_space=pltpu.HBM)
VMEM = pl.BlockSpec(memory_space=pltpu.VMEM)
STATE = [
    jax.ShapeDtypeStruct((KV_HEADS, QROWS, 128), F32),
    jax.ShapeDtypeStruct((KV_HEADS, QROWS, 2 * HEAD_WIDTH), F32),
]
ASKED = jax.ShapeDtypeStruct((KV_HEADS, QROWS, 2 * HEAD_WIDTH), BF16)
PIECE = jax.ShapeDtypeStruct((2 * ROWS, WIDTH), BF16)
ANSWER = pltpu.HBM((ROWS, QUERY_WIDTH), BF16)


def moved(shard, axes, target):
    sizes = [SIZES[a] for a in axes]
    pairs = []
    for source in range(math.prod(sizes)):
        place = [int(i) for i in np.unravel_index(source, sizes)]
        goal = target(*place)
        if goal is not None:
            goal = [a % b for a, b in zip(goal, sizes)]
            pairs.append((source, int(np.ravel_multi_index(goal, sizes))))
    return lax.ppermute(shard, axes if len(axes) > 1 else axes[0], pairs)


def cost(keys):
    return pl.CostEstimate(
        flops=4 * KV_HEADS * QROWS * keys * 256,
        bytes_accessed=keys * WIDTH * 4,
        transcendentals=KV_HEADS * QROWS * keys,
    )


def in_hbm(*arrays):
    return [pltpu.with_memory_space_constraint(a, pltpu.HBM) for a in arrays]


def iota(shape, axis):
    return lax.broadcasted_iota(I32, shape, axis)


def lanes(j):
    return pl.ds(pl.multiple_of(j * HEAD_WIDTH, HEAD_WIDTH), HEAD_WIDTH)


def ask(q_hbm, qa_ref, sem):
    copies = []
    for h in range(KV_HEADS * GROUP_WIDTH):
        source = q_hbm.at[:, pl.ds(h * HEAD_WIDTH, HEAD_WIDTH)]
        j, g = divmod(h, GROUP_WIDTH)
        goal = qa_ref.at[j, pl.ds(g * ROWS, ROWS), pl.ds(0, HEAD_WIDTH)]
        copies.append(pltpu.make_async_copy(source, goal, sem.at[h]))
    return copies


def mark_rows(qa_ref):
    hot = jnp.where(iota((QROWS, 128), 0) % ROWS == iota((QROWS, 128), 1), 1.0, 0.0).astype(BF16)
    for j in range(KV_HEADS):
        qa_ref[j, :, HEAD_WIDTH:] = hot


def score(q, keys, bias):
    wide = jnp.concatenate([keys, bias], axis=1)
    return lax.dot_general(q, wide, (((1,), (1,)), ((), ())), preferred_element_type=F32)


def peak(s):
    parts = [s[:, i : i + 128] for i in range(0, s.shape[1], 128)]
    while len(parts) > 1:
        pairs = [jnp.maximum(a, b) for a, b in zip(parts[::2], parts[1::2])]
        parts = pairs + parts[len(parts) // 2 * 2 :]
    return parts[0]


def spread(column):
    return jnp.broadcast_to(jnp.max(column, axis=1, keepdims=True), (QROWS, 128))


def mix(s, low, values):
    lows = jnp.concatenate([low] * (s.shape[1] // 128), axis=1)
    weights = jnp.exp2(s * TO_LOG2 - lows).astype(BF16)
    wide = jnp.concatenate([values, jnp.ones((values.shape[0], HEAD_WIDTH), BF16)], axis=1)
    return jnp.dot(weights, wide, preferred_element_type=F32)


def attend(j, qa_ref, keys, values, bias, s_ref, m_in, acc_in):
    s = score(qa_ref[j], keys, bias)
    s_ref[j] = s
    column = peak(s)
    if m_in is not None:
        column = jnp.maximum(column, m_in[j])
    top = spread(column)
    low = top * TO_LOG2
    total = mix(s_ref[j], low, values)
    if m_in is not None:
        shrink = jnp.exp2(m_in[j] * TO_LOG2 - low)
        total = total + acc_in[j] * jnp.concatenate([shrink, shrink], axis=1)
    return top, total


def answer(j, total, answer_ref, out_hbm, sems):
    result = (total[:, :HEAD_WIDTH] / total[:, HEAD_WIDTH:]).astype(BF16)
    for g in range(GROUP_WIDTH):
        at = (j * GROUP_WIDTH + g) * HEAD_WIDTH
        answer_ref[:, at : at + HEAD_WIDTH] = result[g * ROWS : (g + 1) * ROWS]
    part = pl.ds(j * GROUP_WIDTH * HEAD_WIDTH, GROUP_WIDTH * HEAD_WIDTH)
    copy = pltpu.make_async_copy(answer_ref.at[:, part], out_hbm.at[:, part], sems.at[j])
    copy.start()
    return copy


ANSWER_SCRATCH = [pltpu.VMEM(ANSWER.shape, BF16), pltpu.SemaphoreType.DMA((KV_HEADS,))]


def prompt_kernel(pieces, first, last, *refs):
    count = len(pieces)
    keys_in_all = count * SIDE * ROWS
    if first:
        q_hbm, *refs = refs
    else:
        qa_ref, m_in, acc_in, *refs = refs
    piece_refs, refs = refs[:count], refs[count:]
    if last:
        out_hbm, *refs = refs
    else:
        m_ref, acc_ref, *refs = refs
    if first:
        qa_ref, *refs = refs
    bias_ref, s_ref, *refs = refs
    if first:
        copies = ask(q_hbm, qa_ref, refs[0])
        for copy in copies:
            copy.start()
        mark_rows(qa_ref)
    x, y, c = lax.axis_index("x"), lax.axis_index("y"), lax.axis_index("c")
    me = x * 8 + y * 2 + c
    row_pos = me * ROWS + iota((ROWS, 128), 1)
    for i, (swapped, k2) in enumerate(pieces):
        core = (1 - c) if swapped else c
        for k1 in range(SIDE):
            on_x = jnp.where(core == 0, k2, k1)
            on_y = jnp.where(core == 0, k1, k2)
            block = ((x - on_x) & 3) * 8 + ((y - on_y) & 3) * 2 + core
            key_pos = block * ROWS + iota((ROWS, 128), 0)
            bias = jnp.where(key_pos > row_pos, -BIG, 0.0).astype(BF16)
            at = (i * SIDE + k1) * ROWS
            bias_ref[at : at + ROWS, :] = bias
    if first:
        for copy in copies:
            copy.wait()

    def piece_rows(half, j):
        head = slice(j * HEAD_WIDTH, (j + 1) * HEAD_WIDTH)
        rows = slice(half * ROWS, (half + 1) * ROWS)
        parts = [ref[:, rows, head].reshape(SIDE * ROWS, HEAD_WIDTH) for ref in piece_refs]
        return jnp.concatenate(parts, axis=0)

    sent = []
    for j in range(KV_HEADS):
        top, total = attend(
            j, qa_ref, piece_rows(0, j), piece_rows(1, j), bias_ref[...], s_ref,
            None if first else m_in, None if first else acc_in,
        )
        if last:
            sent.append(answer(j, total, refs[0], out_hbm, refs[1]))
        else:
            m_ref[j] = top
            acc_ref[j] = total
    for copy in sent:
        copy.wait()


def prompt_attend(arrays, pieces, q=None, state=None, last=False):
    first = state is None
    keys = len(pieces) * SIDE * ROWS
    scratch = [pltpu.VMEM((keys, 128), BF16), pltpu.VMEM((KV_HEADS, QROWS, keys), F32)]
    if first:
        scratch.append(pltpu.SemaphoreType.DMA((KV_HEADS * GROUP_WIDTH,)))
    if last:
        scratch += ANSWER_SCRATCH

    def kernel(*refs):
        prompt_kernel(pieces, first, last, *refs)

    before = in_hbm(q) if first else list(state)
    return pl.pallas_call(
        kernel,
        out_shape=ANSWER if last else STATE + [ASKED] * first,
        in_specs=([HBM] if first else [VMEM] * 3) + [VMEM] * len(pieces),
        out_specs=HBM if last else [VMEM] * (2 + first),
        scratch_shapes=scratch,
        compiler_params=pltpu.CompilerParams(vmem_limit_bytes=VMEM_LIMIT),
        cost_estimate=cost(keys),
    )(*before, *arrays)


def join_kernel(k_hbm, v_hbm, kv_ref, sems):
    copies = [
        pltpu.make_async_copy(part, kv_ref.at[pl.ds(i * ROWS, ROWS)], sems.at[i])
        for i, part in enumerate((k_hbm, v_hbm))
    ]
    for copy in copies:
        copy.start()
    for copy in copies:
        copy.wait()


def join(keys, values):
    return pl.pallas_call(
        join_kernel,
        out_shape=PIECE,
        in_specs=[HBM] * 2,
        out_specs=VMEM,
        scratch_shapes=[pltpu.SemaphoreType.DMA((2,))],
        compiler_params=pltpu.CompilerParams(vmem_limit_bytes=VMEM_LIMIT),
    )(*in_hbm(keys, values))


BLOCK = jax.ShapeDtypeStruct((SIDE, *PIECE.shape), BF16)


def place_kernel(count, *refs):
    parts, outs = refs[:count], refs[count:]
    slots = [out.at[i] for out in outs for i in range(out.shape[0])]
    for i, slot in enumerate(slots):
        slot[...] = parts[i][...] if parts else jnp.zeros(slot.shape, BF16)


def place(parts, counts):
    def kernel(*refs):
        place_kernel(len(parts), *refs)

    return pl.pallas_call(
        kernel,
        out_shape=[pltpu.VMEM((n, *PIECE.shape), BF16) for n in counts],
        in_specs=[VMEM] * len(parts),
        out_specs=[VMEM] * len(counts),
        compiler_params=pltpu.CompilerParams(vmem_limit_bytes=VMEM_LIMIT),
    )(*parts)


def after_kernel(part_ref, state_ref, out_ref):
    out_ref[...] = part_ref[...]


def after(part, state):
    return pl.pallas_call(
        after_kernel,
        out_shape=pltpu.VMEM(part.shape, part.dtype),
        in_specs=[VMEM, VMEM],
        out_specs=VMEM,
        compiler_params=pltpu.CompilerParams(vmem_limit_bytes=VMEM_LIMIT),
    )(part, state)


def pool_kernel(
    len_hbm, table_hbm, owner_hbm, q_hbm, new_k_hbm, new_v_hbm, k_hbm, v_hbm,
    m_ref, acc_ref, qa_ref, hand_bias_ref, pick_ref,
    k_ref, v_ref, new_k_ref, new_v_ref, bias_ref, new_bias_ref, s_ref, new_s_ref, mx_ref,
    len_ref, table_ref, owner_ref, own_ref, sems, cache_sems, ask_sems,
):
    @pl.when(lax.axis_index("s") == 1)
    def _():
        small = [
            pltpu.make_async_copy(len_hbm, len_ref, sems.at[0]),
            pltpu.make_async_copy(table_hbm, table_ref, sems.at[1]),
            pltpu.make_async_copy(owner_hbm, owner_ref, sems.at[2]),
            pltpu.make_async_copy(owner_hbm, own_ref, sems.at[3]),
        ]
        large = ask(q_hbm, qa_ref, ask_sems) + [
            pltpu.make_async_copy(new_k_hbm, new_k_ref.at[pl.ds(0, ROWS)], sems.at[4]),
            pltpu.make_async_copy(new_v_hbm, new_v_ref.at[pl.ds(0, ROWS)], sems.at[5]),
        ]
        half = TOKENS // 2

        def cache_half(i, part):
            source, goal = ((k_hbm, k_ref), (v_hbm, v_ref))[i]
            rows = pl.ds(pl.multiple_of(part * half, half), half)
            return pltpu.make_async_copy(source.at[rows], goal.at[rows], cache_sems.at[i, part])

        for copy in small + large + [cache_half(i, part) for i in range(2) for part in range(2)]:
            copy.start()
        me = lax.axis_index("x") * 8 + lax.axis_index("y") * 2 + lax.axis_index("c")
        mark_rows(qa_ref)
        new_key, new_row = iota((NEW, 128), 0), iota((NEW, 128), 1)
        seen = (new_key // STEPS == new_row // STEPS) & (new_key <= new_row)
        new_bias_ref[...] = jnp.where(seen & (new_key < ROWS), 0.0, -BIG).astype(BF16)
        new_k_ref[ROWS:] = jnp.zeros((NEW - ROWS, WIDTH), BF16)
        new_v_ref[ROWS:] = jnp.zeros((NEW - ROWS, WIDTH), BF16)
        for copy in small:
            copy.wait()
        sequence = iota((8, 128), 1) // STEPS
        length = jnp.zeros((8, 128), I32)
        start = jnp.zeros((8, 128), I32)
        offset = jnp.int32(0)
        for s in range(SEQS):
            one = len_ref[0, s]
            length = jnp.where(sequence == s, one, length)
            start = jnp.where(sequence == s, offset, start)
            offset = offset + ((one + PAGE_TOKENS - 1) >> 3)
        length, start = length[0:1], start[0:1]
        past = iota((PAGES, 128), 0) - start
        live = jnp.where(past >= 0, jnp.clip(length - past * PAGE_TOKENS, 0, PAGE_TOKENS), 0)
        hot = jnp.where(iota((PAGES, PAGES), 0) == table_ref[...], 1.0, 0.0).astype(BF16)
        of_page = jnp.dot(hot, live.astype(F32).astype(BF16), preferred_element_type=F32)
        page = iota((HAND, PROMPT_PAGES), 0)
        same_index = iota((HAND, PROMPT_PAGES), 1) // PPD == page // 2
        named = jnp.zeros((HAND, PROMPT_PAGES), F32)
        for t in range(TOP):
            named = named + jnp.where((owner_ref[t : t + 1] == me) & same_index, 1.0, 0.0)
        total = jnp.sum(named, axis=1, keepdims=True)
        filled = jnp.where(total > (iota((HAND, 1), 0) % 2).astype(F32), 1.0, 0.0)

        def token_bias(tokens, pages):
            wide = jnp.broadcast_to(tokens[:, None, :], (pages, PAGE_TOKENS, 128))
            step = iota((pages, PAGE_TOKENS, 128), 1).astype(F32)
            bias = jnp.where(step < wide, 0.0, -BIG)
            return bias.reshape(pages * PAGE_TOKENS, 128).astype(BF16)

        hand = of_page[:HAND]
        hand_bias_ref[...] = token_bias(hand * filled, HAND)
        bias_ref[0:HAND_TOKENS] = token_bias(hand * (1.0 - filled), HAND)
        bias_ref[HAND_TOKENS:TOKENS] = token_bias(of_page[HAND:], PAGES - HAND)
        lane = iota((8, ROWS), 1)
        owners = [own_ref[i % TOP, me * PPD + i // TOP] for i in range(PPD * TOP)]
        targets = []
        for t in range(TOP):
            target = jnp.zeros((8, ROWS), I32)
            for p in range(PPD):
                i = p * TOP + t
                rank = jnp.int32(0)
                for e in range(i):
                    rank = rank + jnp.where(owners[e] == owners[i], 1, 0)
                target = jnp.where(lane // PAGE_TOKENS == p, owners[i] * 2 + rank, target)
            targets.append(target[0:1])
        slot = iota((HAND_TOKENS, ROWS), 0)
        column = iota((HAND_TOKENS, ROWS), 1)
        to_slot = (slot // PAGE_TOKENS == targets[0]) | (slot // PAGE_TOKENS == targets[1])
        same = slot % PAGE_TOKENS == column % PAGE_TOKENS
        pick_ref[...] = jnp.where(to_slot & same, 1.0, 0.0).astype(BF16)
        for copy in large:
            copy.wait()

        def rows(c):
            return pl.ds(pl.multiple_of(c * CHUNK, CHUNK), CHUNK)

        def one_head(j, carry):
            s = score(qa_ref[j], new_k_ref[:, lanes(j)], new_bias_ref[...])
            new_s_ref[...] = s
            mx_ref[...] = s

            def scores(part, carry):
                @pl.when(j == 0)
                def _():
                    cache_half(0, part).wait()

                for i in range(HALF_CHUNKS):
                    c = part * HALF_CHUNKS + i
                    s = score(qa_ref[j], k_ref[rows(c), lanes(j)], bias_ref[rows(c)])
                    s_ref[c] = s
                    mx_ref[...] = jnp.maximum(mx_ref[...], peak(s))
                return carry

            lax.fori_loop(0, 2, scores, 0)
            top = spread(mx_ref[...])
            m_ref[j] = top
            mx_ref[...] = top * TO_LOG2
            acc_ref[j] = mix(new_s_ref[...], mx_ref[...], new_v_ref[:, lanes(j)])

            def mixes(part, carry):
                @pl.when(j == 0)
                def _():
                    cache_half(1, part).wait()

                for i in range(HALF_CHUNKS):
                    c = part * HALF_CHUNKS + i
                    acc_ref[j] += mix(s_ref[c], mx_ref[...], v_ref[rows(c), lanes(j)])
                return carry

            lax.fori_loop(0, 2, mixes, 0)
            return carry

        lax.fori_loop(0, KV_HEADS, one_head, 0)


def pool_attend(lengths, table, owners, q, new_k, new_v, cache_k, cache_v):
    return pl.pallas_call(
        pool_kernel,
        out_shape=STATE
        + [
            ASKED,
            jax.ShapeDtypeStruct((HAND_TOKENS, 128), BF16),
            jax.ShapeDtypeStruct((HAND_TOKENS, ROWS), BF16),
        ],
        in_specs=[HBM] * 8,
        out_specs=[VMEM] * 5,
        scratch_shapes=[
            pltpu.VMEM((TOKENS, WIDTH), BF16),
            pltpu.VMEM((TOKENS, WIDTH), BF16),
            pltpu.VMEM((NEW, WIDTH), BF16),
            pltpu.VMEM((NEW, WIDTH), BF16),
            pltpu.VMEM((TOKENS, 128), BF16),
            pltpu.VMEM((NEW, 128), BF16),
            pltpu.VMEM((TOKENS // CHUNK, QROWS, CHUNK), F32),
            pltpu.VMEM((QROWS, NEW), F32),
            pltpu.VMEM((QROWS, 128), F32),
            pltpu.SMEM((1, SEQS), I32),
            pltpu.VMEM((1, PAGES), I32),
            pltpu.VMEM((TOP, PROMPT_PAGES), I32),
            pltpu.SMEM((TOP, PROMPT_PAGES), I32),
            pltpu.SemaphoreType.DMA((6,)),
            pltpu.SemaphoreType.DMA((2, 2)),
            pltpu.SemaphoreType.DMA((KV_HEADS * GROUP_WIDTH,)),
        ],
        compiler_params=pltpu.CompilerParams(vmem_limit_bytes=POOL_LIMIT),
        cost_estimate=cost(TOKENS + NEW),
    )(*in_hbm(lengths, table, owners, q, new_k, new_v, cache_k, cache_v))


def pick_kernel(pick_ref, kv_ref, out_ref):
    for i in range(2):
        part = kv_ref[i * ROWS : (i + 1) * ROWS]
        rows = jnp.dot(pick_ref[...], part, preferred_element_type=F32).astype(BF16)
        out_ref[:, i] = rows.reshape(HAND // 2, 2 * PAGE_TOKENS, WIDTH)


def pick_pages(pick, kv):
    return pl.pallas_call(
        pick_kernel,
        out_shape=jax.ShapeDtypeStruct((HAND // 2, 2, 2 * PAGE_TOKENS, WIDTH), BF16),
        in_specs=[VMEM, VMEM],
        out_specs=VMEM,
        compiler_params=pltpu.CompilerParams(vmem_limit_bytes=VMEM_LIMIT),
    )(pick, kv)


def hand_kernel(arrived_ref, bias_ref, qa_ref, m_in, acc_in, out_hbm, s_ref, answer_ref, sems):
    sent = []
    for j in range(KV_HEADS):
        head = slice(j * HEAD_WIDTH, (j + 1) * HEAD_WIDTH)
        _, total = attend(
            j, qa_ref,
            arrived_ref[:, 0, :, head].reshape(HAND_TOKENS, HEAD_WIDTH),
            arrived_ref[:, 1, :, head].reshape(HAND_TOKENS, HEAD_WIDTH),
            bias_ref[...], s_ref, m_in, acc_in,
        )
        sent.append(answer(j, total, answer_ref, out_hbm, sems))
    for copy in sent:
        copy.wait()


def hand_attend(arrived, bias, qa, m, acc):
    return pl.pallas_call(
        hand_kernel,
        out_shape=ANSWER,
        in_specs=[VMEM] * 5,
        out_specs=HBM,
        scratch_shapes=[pltpu.VMEM((KV_HEADS, QROWS, HAND_TOKENS), F32)] + ANSWER_SCRATCH,
        compiler_params=pltpu.CompilerParams(vmem_limit_bytes=VMEM_LIMIT),
        cost_estimate=cost(HAND_TOKENS),
    )(arrived, bias, qa, m, acc)


def body(
    queries, keys, values, page_owner, lengths, page_table, group_cache_keys, group_cache_values
):
    first_section = lax.axis_index("s") == 0
    q = queries[0]

    def shifted(part, k, swap):
        def target(x, y, c):
            return (x, y + k, c) if (c == 0) != swap else (x + k, y, c)

        return moved(part, CTX, target)

    def other_core(part):
        return moved(part, ("c",), lambda c: (1 - c,))

    def next_ones(keys, values):
        kv = join(keys, values)
        return tuple(place([kv, kv, shifted(kv, 1, False), shifted(kv, 3, False)], [1, 3]))

    kv, three = lax.cond(
        first_section, next_ones, lambda *_: tuple(place([], [1, 3])), keys[0], values[0]
    )
    crossed = moved(kv[0], ("s",), lambda s: (1,) if s == 0 else None)

    def the_last(three):
        kv, near, back = three[0], three[1], three[2]
        return place([kv, near, shifted(near, 1, False), back], [SIDE])[0]

    block = lax.cond(first_section, the_last, lambda *_: place([], [SIDE])[0], three)
    ready = pool_attend(
        lengths, page_table, page_owner.T, q, keys[0], values[0],
        group_cache_keys.reshape(TOKENS, WIDTH), group_cache_values.reshape(TOKENS, WIDTH),
    )

    def prompt(q, block, crossed, *_):
        block_other = other_core(block)
        h = HOPS
        far = [shifted(block, k, True) for k in h]
        m, acc, qa = prompt_attend([block, block_other], [(False, 0), (True, 0)], q=q)
        far_other = []
        for i in range(2):
            far[i], m, acc = lax.optimization_barrier((far[i], m, acc))
            far_other.append(other_core(far[i]))
        m, acc = prompt_attend(
            [far[0], far[1], far_other[0]], [(False, h[0]), (False, h[1]), (True, h[0])],
            state=(qa, m, acc),
        )
        last = far[2]
        far_other.append(other_core(last))
        m, acc = prompt_attend(
            [far_other[1], last], [(True, h[1]), (False, h[2])], state=(qa, m, acc)
        )
        return prompt_attend([far_other[2]], [(True, h[2])], state=(qa, m, acc), last=True)

    def decode(q, block, crossed, m, acc, qa, hand_bias, pick):
        outgoing = pick_pages(pick, crossed)
        arrived = lax.all_to_all(outgoing, CTX, 0, 0, tiled=True)
        return hand_attend(arrived, hand_bias, qa, m, acc)

    out = lax.cond(first_section, prompt, decode, q, block, crossed, *ready)
    return out[None]


def solution(mesh):
    inner = Mesh(mesh.devices.reshape([SIZES[a] for a in AXES]), AXES)
    return jax.shard_map(
        body,
        mesh=inner,
        in_specs=(
            P("s", CTX, "t"),
            P("s", CTX, "t"),
            P("s", CTX, "t"),
            P(),
            P(CTX, None),
            P(CTX, None),
            P(CTX, None, "t"),
            P(CTX, None, "t"),
        ),
        out_specs=P("s", CTX, "t"),
        check_vma=False,
    )
```
